32 devices in a mesh: row: 8 (over z, y), col: 4 (over x, core).
Axes of the slice: x: 2, y: 2, z: 4, core: 2. Of those that a mesh axis runs over, the one named last changes fastest.
Arguments:
- features: bfloat16 [2048, 512], P(('row', 'col')), may hold values from -6 to 6
- w_first: bfloat16 [512, 512], replicated, may hold values from -0.25 to 0.25
- w_second: bfloat16 [512, 512], replicated, may hold values from -0.25 to 0.25
- block_index: int32 [8, 4, 8], P('row', 'col'), may hold values from 0 to 7, as said below
- block_count: int32 [8, 4], P('row', 'col'), may hold values from 0 to 2, as said below
- block_values: bfloat16 [8, 4, 8, 128, 128], P('row', 'col'), may hold values from -0.4375 to 0.4375
- cotangent: bfloat16 [2048, 512], P(('row', 'col')), may hold values from -0.125 to 0.125
Outputs:
- out_second: bfloat16 [2048, 512], P(('row', 'col'))
- grad_first: float32 [512, 512], replicated
- grad_second: float32 [512, 512], replicated
The draws below stay inside these ranges and needn't reach their ends.
Inputs may be any that keep to these rules, and one draw needn't show every extreme that they name: `block_index`: in each tile the 8 slots name every block position p = r * 4 + c (block row r, block column c of the tile) once, in some order; the first block_count slots are the tile's nonzero blocks and the others are unused. `block_count`: nonzero blocks of each tile; in every draw some tile has exactly 2.
All inputs are finite; a program needn't handle non-finite values.
Results may differ from the reference program's by a relative error of at most 0.0061.
Values may be sent and summed in bfloat16 or wider, within the bound.
No kernel may reach another device: no remote copies, remote signals or barrier semaphores. Data moves between devices by JAX's collectives and lax.ppermute only.
A program may use at most 64 MiB of HBM per device.

```python
import jax
import jax.numpy as jnp
from jax import lax

WIDTH = 512
BLOCK = 128
ROW_TILES = 8
COL_TILES = 4
NODES = 2048
TILE_ROWS = 256
TILE_COLS = 512
BLK_ROWS = 2
BLK_COLS = 4
SLOTS = 8
MAX_BLOCKS = 2
N_ROW = 8
N_COL = 4


def tile_pattern(key):
    base = jax.random.fold_in(key, 4099)
    key_rows, key_cols, key_roll, key_full, key_order = jax.random.split(base, 5)
    brow_total = ROW_TILES * BLK_ROWS
    bcol_total = COL_TILES * BLK_COLS
    level_rows = jax.random.randint(key_rows, (brow_total,), 1, 5, dtype=jnp.int32)
    level_cols = jax.random.randint(key_cols, (bcol_total,), 1, 5, dtype=jnp.int32)
    roll = jax.random.randint(key_roll, (brow_total, bcol_total), 0, 64, dtype=jnp.int32)
    present = (roll < level_rows[:, None] * level_cols[None, :]).astype(jnp.int32)
    present = present.reshape(ROW_TILES, BLK_ROWS, COL_TILES, BLK_COLS)
    present = present.transpose(0, 2, 1, 3).reshape(ROW_TILES, COL_TILES, SLOTS)
    chosen = jax.random.randint(key_full, (), 0, ROW_TILES * COL_TILES, dtype=jnp.int32)
    tile_ident = jnp.arange(ROW_TILES, dtype=jnp.int32)[:, None] * COL_TILES + jnp.arange(COL_TILES, dtype=jnp.int32)[None, :]
    present = jnp.where((tile_ident == chosen)[:, :, None], 1, present)
    shuffle = jax.random.randint(key_order, (ROW_TILES, COL_TILES, SLOTS), 0, SLOTS, dtype=jnp.int32)
    position = jnp.arange(SLOTS, dtype=jnp.int32)
    score = (1 - present) * (SLOTS * SLOTS) + shuffle * SLOTS + position[None, None, :]
    order = jnp.argsort(score, axis=-1, stable=True).astype(jnp.int32)
    totals = jnp.minimum(jnp.sum(present, axis=-1), MAX_BLOCKS).astype(jnp.int32)
    return (order, totals)


def draw_block_index(key, part):
    return tile_pattern(key)[0]


def draw_block_count(key, part):
    return tile_pattern(key)[1]


def block_scale(own_key, shape, cuts, least, high):
    gain = 1.0
    for dim, blocks in cuts:
        steps = jax.random.uniform(jax.random.fold_in(jax.random.fold_in(own_key, 6), dim), (blocks,), jnp.float32, least / len(cuts), high / len(cuts))
        gain = gain * jnp.repeat(jnp.exp(steps), shape[dim] // blocks).reshape((-1,) + (1,) * (len(shape) - 1 - dim))
    return gain


def centred(own_key, dims, scale, limit, cuts=(), held_as=jnp.bfloat16):
    array = scale * jax.random.normal(own_key, dims, jnp.float32)
    if cuts:
        array = array * block_scale(own_key, dims, cuts, -0.22, 0.18)
    return jnp.clip(array, -limit, limit).astype(held_as)


def setup_inputs(seed: int = 0) -> dict:
    key_list = jax.random.split(jax.random.key(seed), 8)
    return {
        "features": centred(key_list[0], (NODES, WIDTH), 1.0, 6.0, ((0, 32),)),
        "w_first": centred(key_list[1], (WIDTH, WIDTH), WIDTH ** -0.5, 0.25),
        "w_second": centred(key_list[2], (WIDTH, WIDTH), WIDTH ** -0.5, 0.25),
        "block_index": draw_block_index(jax.random.fold_in(key_list[7], 71), 0),
        "block_count": draw_block_count(jax.random.fold_in(key_list[7], 71), 0),
        "block_values": centred(key_list[5], (ROW_TILES, COL_TILES, SLOTS, BLOCK, BLOCK), (max(NODES // 10, BLOCK)) ** -0.5, 0.4375, ((0, 8), (1, 4))),
        "cotangent": centred(key_list[6], (NODES, WIDTH), NODES ** -0.5, 0.125, ((0, 32),)),
    }


def activate(v):
    return jax.nn.gelu(v, approximate=True)

def tile_term(tile_values, slot_index, slot_count, panel_part, flip):
    is_live = jnp.arange(SLOTS, dtype=jnp.int32) < slot_count
    block_row = slot_index // BLK_COLS
    block_col = slot_index % BLK_COLS
    values_wide = tile_values.astype(jnp.float32)
    feat_width = panel_part.shape[1]
    if flip:
        picked = panel_part.reshape(BLK_ROWS, BLOCK, feat_width)[block_row].astype(jnp.float32)
        product = jnp.einsum('sab,saf->sbf', values_wide, picked, precision=lax.Precision.HIGHEST)
        target = block_col
        out_blocks = BLK_COLS
    else:
        picked = panel_part.reshape(BLK_COLS, BLOCK, feat_width)[block_col].astype(jnp.float32)
        product = jnp.einsum('sab,sbf->saf', values_wide, picked, precision=lax.Precision.HIGHEST)
        target = block_row
        out_blocks = BLK_ROWS
    targets = jnp.arange(out_blocks, dtype=jnp.int32)
    onehot = ((target[None, :] == targets[:, None]) & is_live[None, :]).astype(jnp.float32)
    term = jnp.einsum('os,saf->oaf', onehot, product, precision=lax.Precision.HIGHEST)
    return term.reshape(out_blocks * BLOCK, feat_width)

def aggregate(block_values, block_index, block_count, panel, flip):
    feat_width = panel.shape[1]
    if flip:
        outer_count, inner_count, out_rows = (N_COL, N_ROW, TILE_COLS)
    else:
        outer_count, inner_count, out_rows = (N_ROW, N_COL, TILE_ROWS)

    def band(outer_no):

        def add(total, inner_no):
            if flip:
                row_no, col_no = (inner_no, outer_no)
                part = lax.dynamic_slice_in_dim(panel, (row_no * TILE_ROWS).astype(jnp.int32), TILE_ROWS, 0)
            else:
                row_no, col_no = (outer_no, inner_no)
                part = lax.dynamic_slice_in_dim(panel, (col_no * TILE_COLS).astype(jnp.int32), TILE_COLS, 0)
            term = tile_term(block_values[row_no, col_no], block_index[row_no, col_no], block_count[row_no, col_no], part, flip)
            return (total + term, None)
        total, _ = lax.scan(add, jnp.zeros((out_rows, feat_width), jnp.float32), jnp.arange(inner_count, dtype=jnp.int32))
        return total
    bands = lax.map(band, jnp.arange(outer_count, dtype=jnp.int32))
    return bands.reshape(NODES, feat_width)

def reference(features, w_first, w_second, block_index, block_count, block_values, cotangent):
    first_linear = jnp.dot(features, w_first, preferred_element_type=jnp.float32).astype(jnp.bfloat16)
    first_sum = aggregate(block_values, block_index, block_count, first_linear, True)
    first_value, act_back = jax.vjp(activate, first_sum)
    first_active = first_value.astype(jnp.bfloat16)
    second_linear = jnp.dot(first_active, w_second, preferred_element_type=jnp.float32).astype(jnp.bfloat16)
    out_second = aggregate(block_values, block_index, block_count, second_linear, False).astype(jnp.bfloat16)
    back_second = aggregate(block_values, block_index, block_count, cotangent, True).astype(jnp.bfloat16)
    grad_second = jnp.dot(first_active.T, back_second, preferred_element_type=jnp.float32)
    back_act = jnp.dot(back_second, w_second.T, preferred_element_type=jnp.float32)
    back_first = act_back(back_act)[0].astype(jnp.bfloat16)
    back_linear = aggregate(block_values, block_index, block_count, back_first, False).astype(jnp.bfloat16)
    grad_first = jnp.dot(features.T, back_linear, preferred_element_type=jnp.float32)
    return (out_second, grad_first, grad_second)
```

```python
import functools
import math

import jax
import jax.numpy as jnp
from jax import lax
from jax.experimental import pallas as pl
from jax.experimental.pallas import tpu as pltpu
from jax.sharding import PartitionSpec as P

AXES = ("row", "col")
GELU_C = 0.7978845608028654
GELU_A = 0.044715
REPLICATE_BYTES = 8 * 1024 * 1024


def activate(v):
    return jax.nn.gelu(v, approximate=True)


def combine(tile_values, slot_index, slot_count, full_panel, flip):
    slots = slot_index.shape[0]
    block_size = tile_values.shape[-1]
    feat_width = full_panel.shape[1]
    in_blocks = full_panel.shape[0] // block_size
    if flip:
        col_blocks = slots // in_blocks
        out_blocks = col_blocks
    else:
        col_blocks = in_blocks
        out_blocks = slots // in_blocks
    group_size = math.gcd(slots, 32)
    panel_blocks = full_panel.reshape(in_blocks, block_size, feat_width)
    targets = jnp.arange(out_blocks, dtype=jnp.int32)
    offsets = jnp.arange(group_size, dtype=jnp.int32)

    def add_group(group_no, total):
        first_slot = group_no * group_size
        slot_ids = lax.dynamic_slice_in_dim(slot_index, first_slot, group_size, 0)
        group_values = lax.dynamic_slice_in_dim(tile_values, first_slot, group_size, 0)
        block_row = slot_ids // col_blocks
        block_col = slot_ids % col_blocks
        if flip:
            picked = panel_blocks[block_row]
            product = jnp.einsum(
                "sab,saf->sbf", group_values, picked, preferred_element_type=jnp.float32
            )
            target = block_col
        else:
            picked = panel_blocks[block_col]
            product = jnp.einsum(
                "sab,sbf->saf", group_values, picked, preferred_element_type=jnp.float32
            )
            target = block_row
        is_live = first_slot + offsets < slot_count
        onehot = ((target[None, :] == targets[:, None]) & is_live[None, :]).astype(jnp.float32)
        return total + jnp.einsum("os,saf->oaf", onehot, product, precision=lax.Precision.HIGHEST)

    groups = (slot_count + group_size - 1) // group_size
    total = lax.fori_loop(
        0, groups, add_group, jnp.zeros((out_blocks, block_size, feat_width), jnp.float32)
    )
    return total.reshape(out_blocks * block_size, feat_width)


def spread_rows(layer_input, tile_values, slot_index, slot_count):
    full_panel = lax.all_gather(layer_input, "row", axis=0, tiled=True)
    partial_value = combine(tile_values, slot_index, slot_count, full_panel, False)
    return lax.psum_scatter(partial_value, "col", scatter_dimension=0, tiled=True)


def spread_cols(layer_input, tile_values, slot_index, slot_count):
    full_panel = lax.all_gather(layer_input, "col", axis=0, tiled=True)
    partial_value = combine(tile_values, slot_index, slot_count, full_panel, True)
    return lax.psum_scatter(partial_value, "row", scatter_dimension=0, tiled=True)


def tiled_local(features, w_first, w_second, block_index, block_count, block_values, cotangent):
    slot_index = block_index[0, 0]
    slot_count = block_count[0, 0]
    tile_values = block_values[0, 0]
    feat_width = features.shape[1]
    first_linear = jnp.dot(features, w_first, preferred_element_type=jnp.float32).astype(
        jnp.bfloat16
    )
    joined = jnp.concatenate([first_linear, cotangent], axis=1)
    summed = spread_cols(joined, tile_values, slot_index, slot_count)
    first_sum = summed[:, :feat_width]
    back_second = summed[:, feat_width:].astype(jnp.bfloat16)
    first_value, act_back = jax.vjp(activate, first_sum)
    first_active = first_value.astype(jnp.bfloat16)
    second_linear = jnp.dot(first_active, w_second, preferred_element_type=jnp.float32).astype(
        jnp.bfloat16
    )
    out_second = spread_rows(second_linear, tile_values, slot_index, slot_count).astype(
        jnp.bfloat16
    )
    second_terms = jnp.einsum(
        "nf,ng->fg", first_active, back_second, preferred_element_type=jnp.float32
    )
    back_act = jnp.einsum("ng,fg->nf", back_second, w_second, preferred_element_type=jnp.float32)
    back_first = act_back(back_act)[0].astype(jnp.bfloat16)
    back_linear = spread_rows(back_first, tile_values, slot_index, slot_count).astype(jnp.bfloat16)
    first_terms = jnp.einsum("nf,ng->fg", features, back_linear, preferred_element_type=jnp.float32)
    grad_first, grad_second = lax.psum((first_terms, second_terms), ("row", "col"))
    return (out_second, grad_first, grad_second)


class Sizes:
    def __init__(self, mesh, features, block_values):
        self.n_row, self.n_col = mesh.shape["row"], mesh.shape["col"]
        self.n_dev = self.n_row * self.n_col
        self.rows, self.width = features.shape[0] // self.n_dev, features.shape[1]
        self.slots, self.block = block_values.shape[2], block_values.shape[-1]
        self.live = self.slots // 4
        self.nodes = features.shape[0]
        self.blk_rows = self.nodes // self.n_row // self.block
        self.blk_cols = self.nodes // self.n_col // self.block
        self.chunks = self.width // self.block
        self.part = self.chunks * self.rows
        self.at_cot = self.part
        self.at_val = 2 * self.part
        self.at_info = self.at_val + self.live * self.block
        self.payload = self.at_info + 16
        self.n_blocks = self.nodes // self.block

    def replicates(self):
        whole = self.n_dev * self.payload * self.block * 2
        return (
            whole <= REPLICATE_BYTES
            and self.n_col == 4
            and self.n_row % 2 == 0
            and 2 * self.rows == self.block
            and self.blk_rows == 2
            and self.n_blocks % 2 == 0
        )


def pack_kernel(sz, index_ref, count_ref, feat_ref, cot_ref, val_ref, out_ref):
    for k in range(sz.chunks):
        lanes = pl.ds(k * sz.block, sz.block)
        out_ref[pl.ds(k * sz.rows, sz.rows), :] = feat_ref[:, lanes]
        out_ref[pl.ds(sz.at_cot + k * sz.rows, sz.rows), :] = cot_ref[:, lanes]
    for s in range(sz.live):
        out_ref[pl.ds(sz.at_val + s * sz.block, sz.block), :] = val_ref[0, 0, s]
    lane = lax.broadcasted_iota(jnp.int32, (16, sz.block), 1)
    info = jnp.where(lane == 0, count_ref[0, 0], 0)
    for s in range(sz.live):
        info = jnp.where(lane == s + 1, index_ref[0, 0, s], info)
    out_ref[pl.ds(sz.at_info, 16), :] = info.astype(jnp.float32).astype(jnp.bfloat16)


def pack(sz, features, block_index, block_count, block_values, cotangent):
    vmem = pl.BlockSpec(memory_space=pltpu.VMEM)
    smem = pl.BlockSpec(memory_space=pltpu.SMEM)
    return pl.pallas_call(
        functools.partial(pack_kernel, sz),
        grid=(1,),
        out_shape=jax.ShapeDtypeStruct((sz.payload, sz.block), jnp.bfloat16),
        in_specs=[
            smem,
            smem,
            pl.BlockSpec((sz.rows, sz.width), lambda i: (0, 0)),
            pl.BlockSpec((sz.rows, sz.width), lambda i: (0, 0)),
            pl.BlockSpec((1, 1, sz.live, sz.block, sz.block), lambda i: (0, 0, 0, 0, 0)),
        ],
        out_specs=pl.BlockSpec((sz.payload, sz.block), lambda i: (0, 0)),
    )(block_index, block_count, features, cotangent, block_values)


def gather_parts(sz, payload):
    n_z = sz.n_row // 2

    def send(value, to):
        pairs = []
        for z in range(n_z):
            for y in range(2):
                for x in range(2):
                    for c in range(2):
                        z2, y2, x2, c2 = to(z, y, x, c)
                        src = (z * 2 + y) * 4 + x * 2 + c
                        pairs.append((src, (z2 * 2 + y2) * 4 + x2 * 2 + c2))
        return lax.ppermute(value, AXES, pairs)

    def first_way(z, y, x, c):
        return (z, y, 1 - x, c) if c == 0 else (z, 1 - y, x, c)

    def second_way(z, y, x, c):
        return (z, 1 - y, x, c) if c == 0 else (z, y, 1 - x, c)

    def sibling(z, y, x, c):
        return (z, y, x, 1 - c)

    shifts = sorted(range(n_z), key=lambda d: min(d, n_z - d))
    parts = []
    for d in shifts:
        own = payload
        if d:
            own = send(payload, lambda z, y, x, c: ((z + d) % n_z, y, x, c))
        near = jnp.concatenate([own, send(own, first_way)], axis=0)
        far = send(near, second_way)
        parts.append((d, near, far, send(near, sibling), send(far, sibling)))
    return parts


def main_kernel(sz, shifts, *refs):
    n_parts = 4 * len(shifts)
    part_refs = refs[:n_parts]
    w1_ref, w2_ref, out_ref, gf_ref, gs_ref = refs[n_parts : n_parts + 5]
    buf, info_v, info_s, fct, gb, act, w1t, rows_out, sem, info_sem = refs[n_parts + 5 :]
    n_z = sz.n_row // 2
    block, width = sz.block, sz.width
    row, col = lax.axis_index("row"), lax.axis_index("col")
    z, y, x, c = row // 2, row % 2, col // 2, col % 2

    copies = []
    for n, d in enumerate(shifts):
        for q in range(4):
            for k in range(2):
                core = c if q < 2 else 1 - c
                first, second = k, q % 2
                dx = jnp.where(core == 0, first, second)
                dy = jnp.where(core == 0, second, first)
                from_z = lax.rem(z + n_z - d, n_z)
                from_y, from_x = lax.rem(y + dy, 2), lax.rem(x + dx, 2)
                dev = (from_z * 2 + from_y) * 4 + from_x * 2 + core
                copy = pltpu.make_async_copy(
                    part_refs[4 * n + q].at[pl.ds(k * sz.payload, sz.payload)],
                    buf.at[dev],
                    sem.at[(4 * n + q) * 2 + k],
                )
                copy.start()
                copies.append(copy)

    w1t[...] = jnp.transpose(w1_ref[...].astype(jnp.float32)).astype(jnp.bfloat16)
    gb[...] = jnp.zeros_like(gb)
    for copy in copies:
        copy.wait()

    for t in range(sz.n_dev):
        line = buf[t, pl.ds(sz.at_info, 16), :]
        info_v[pl.ds(t * 8, 8), :] = line.astype(jnp.float32).astype(jnp.int32)[0:8]
    info_copy = pltpu.make_async_copy(info_v, info_s, info_sem)
    info_copy.start()
    info_copy.wait()

    def tile_blocks(t):
        count = info_s[t * 8, 0]
        for s in range(sz.live):
            p = info_s[t * 8, s + 1]
            yield s < count, p // sz.blk_cols, lax.rem(p, sz.blk_cols), s

    def values(t, s):
        return buf[t, pl.ds(sz.at_val + s * block, block), :]

    def tile_row(i, carry):
        for r in range(sz.blk_rows):
            t0 = i * sz.n_col + 2 * r
            for k in range(2 * sz.chunks):
                at = pl.ds(k * sz.rows, sz.rows)
                piece = jnp.concatenate([buf[t0, at, :], buf[t0 + 1, at, :]], axis=0)
                fct[r, pl.ds(k * block, block), :] = jnp.transpose(piece)
        for j in range(sz.n_col):
            t = i * sz.n_col + j
            for live, r, cb, s in tile_blocks(t):

                @pl.when(live)
                def _():
                    gb[j * sz.blk_cols + cb] += jnp.dot(
                        fct[r], values(t, s), preferred_element_type=jnp.float32
                    )

        return carry

    lax.fori_loop(0, sz.n_row, tile_row, 0)

    def chunk(n, carry):
        both = jnp.concatenate(
            [gb[2 * n].astype(jnp.bfloat16), gb[2 * n + 1].astype(jnp.bfloat16)], axis=1
        )
        g, b = both[:width], both[width:]
        v = jnp.dot(w1t[...], g, preferred_element_type=jnp.float32)
        sq = v * v
        t = jnp.tanh(GELU_C * (v + GELU_A * sq * v))
        half = 0.5 * (1.0 + t)
        a = (v * half).astype(jnp.bfloat16)
        slope = half + 0.5 * v * (1.0 - t * t) * (GELU_C * (1.0 + 3.0 * GELU_A * sq))
        act[2 * n] = a[:, :block]
        act[2 * n + 1] = a[:, block:]
        back = jnp.dot(w2_ref[...], b, preferred_element_type=jnp.float32)
        bf = (back * slope).astype(jnp.bfloat16)
        nt = (((1,), (1,)), ((), ()))
        gs = lax.dot_general(a, b, nt, preferred_element_type=jnp.float32)
        gf = lax.dot_general(g, bf, nt, preferred_element_type=jnp.float32)

        @pl.when(n == 0)
        def _():
            gs_ref[...] = gs
            gf_ref[...] = gf

        @pl.when(n > 0)
        def _():
            gs_ref[...] += gs
            gf_ref[...] += gf

        return carry

    lax.fori_loop(0, sz.n_blocks // 2, chunk, 0)

    rows_out[...] = jnp.zeros_like(rows_out)
    for j in range(sz.n_col):
        t = row * sz.n_col + j
        for live, r, cb, s in tile_blocks(t):

            @pl.when(live & (r == x))
            def _():
                rows_out[...] += lax.dot_general(
                    act[j * sz.blk_cols + cb],
                    values(t, s),
                    (((1,), (1,)), ((), ())),
                    preferred_element_type=jnp.float32,
                )

    h = jnp.transpose(rows_out[...])
    high = h.astype(jnp.bfloat16)
    low = (h - high.astype(jnp.float32)).astype(jnp.bfloat16)
    out = jnp.dot(high, w2_ref[...], preferred_element_type=jnp.float32)
    out += jnp.dot(low, w2_ref[...], preferred_element_type=jnp.float32)
    out = jnp.where(c == 0, out[: sz.rows], out[sz.rows :])
    out_ref[...] = out.astype(jnp.bfloat16)


def replicated_local(sz, features, w_first, w_second, block_index, block_count, block_values, cotangent):
    payload = pack(sz, features, block_index, block_count, block_values, cotangent)
    parts = gather_parts(sz, payload)
    shifts = [p[0] for p in parts]
    arrays = [a for p in parts for a in p[1:]]
    vmem = pl.BlockSpec(memory_space=pltpu.VMEM)
    grad = jax.ShapeDtypeStruct((sz.width, sz.width), jnp.float32)
    return tuple(
        pl.pallas_call(
            functools.partial(main_kernel, sz, shifts),
            out_shape=(jax.ShapeDtypeStruct((sz.rows, sz.width), jnp.bfloat16), grad, grad),
            in_specs=[pl.BlockSpec(memory_space=pl.ANY)] * len(arrays) + [vmem] * 2,
            out_specs=(vmem, vmem, vmem),
            scratch_shapes=[
                pltpu.VMEM((sz.n_dev, sz.payload, sz.block), jnp.bfloat16),
                pltpu.VMEM((sz.n_dev * 8, sz.block), jnp.int32),
                pltpu.SMEM((sz.n_dev * 8, sz.block), jnp.int32),
                pltpu.VMEM((sz.blk_rows, 2 * sz.width, sz.block), jnp.bfloat16),
                pltpu.VMEM((sz.n_blocks, 2 * sz.width, sz.block), jnp.float32),
                pltpu.VMEM((sz.n_blocks, sz.width, sz.block), jnp.bfloat16),
                pltpu.VMEM((sz.width, sz.width), jnp.bfloat16),
                pltpu.VMEM((sz.width, sz.block), jnp.float32),
                pltpu.SemaphoreType.DMA((2 * len(arrays),)),
                pltpu.SemaphoreType.DMA,
            ],
            compiler_params=pltpu.CompilerParams(vmem_limit_bytes=40 * 1024 * 1024),
        )(*arrays, w_first, w_second)
    )


def solution(mesh):
    specs = dict(
        mesh=mesh,
        in_specs=(
            P(("row", "col"), None),
            P(),
            P(),
            P("row", "col", None),
            P("row", "col"),
            P("row", "col", None, None, None),
            P(("row", "col"), None),
        ),
        out_specs=(P(("row", "col"), None), P(), P()),
        check_vma=False,
    )

    def run(features, w_first, w_second, block_index, block_count, block_values, cotangent):
        sz = Sizes(mesh, features, block_values)
        local = functools.partial(replicated_local, sz) if sz.replicates() else tiled_local
        return jax.shard_map(local, **specs)(
            features, w_first, w_second, block_index, block_count, block_values, cotangent
        )

    return run
```

```python
import functools
import math

import jax
import jax.numpy as jnp
from jax import lax
from jax.experimental import pallas as pl
from jax.experimental.pallas import tpu as pltpu
from jax.sharding import PartitionSpec as P

AXES = ("row", "col")
GELU_C = 0.7978845608028654
GELU_A = 0.044715
REPLICATE_BYTES = 8 * 1024 * 1024


def activate(v):
    return jax.nn.gelu(v, approximate=True)


def combine(tile_values, slot_index, slot_count, full_panel, flip):
    slots = slot_index.shape[0]
    block_size = tile_values.shape[-1]
    feat_width = full_panel.shape[1]
    in_blocks = full_panel.shape[0] // block_size
    if flip:
        col_blocks = slots // in_blocks
        out_blocks = col_blocks
    else:
        col_blocks = in_blocks
        out_blocks = slots // in_blocks
    group_size = math.gcd(slots, 32)
    panel_blocks = full_panel.reshape(in_blocks, block_size, feat_width)
    targets = jnp.arange(out_blocks, dtype=jnp.int32)
    offsets = jnp.arange(group_size, dtype=jnp.int32)

    def add_group(group_no, total):
        first_slot = group_no * group_size
        slot_ids = lax.dynamic_slice_in_dim(slot_index, first_slot, group_size, 0)
        group_values = lax.dynamic_slice_in_dim(tile_values, first_slot, group_size, 0)
        block_row = slot_ids // col_blocks
        block_col = slot_ids % col_blocks
        if flip:
            picked = panel_blocks[block_row]
            product = jnp.einsum(
                "sab,saf->sbf", group_values, picked, preferred_element_type=jnp.float32
            )
            target = block_col
        else:
            picked = panel_blocks[block_col]
            product = jnp.einsum(
                "sab,sbf->saf", group_values, picked, preferred_element_type=jnp.float32
            )
            target = block_row
        is_live = first_slot + offsets < slot_count
        onehot = ((target[None, :] == targets[:, None]) & is_live[None, :]).astype(jnp.float32)
        return total + jnp.einsum("os,saf->oaf", onehot, product, precision=lax.Precision.HIGHEST)

    groups = (slot_count + group_size - 1) // group_size
    total = lax.fori_loop(
        0, groups, add_group, jnp.zeros((out_blocks, block_size, feat_width), jnp.float32)
    )
    return total.reshape(out_blocks * block_size, feat_width)


def spread_rows(layer_input, tile_values, slot_index, slot_count):
    full_panel = lax.all_gather(layer_input, "row", axis=0, tiled=True)
    partial_value = combine(tile_values, slot_index, slot_count, full_panel, False)
    return lax.psum_scatter(partial_value, "col", scatter_dimension=0, tiled=True)


def spread_cols(layer_input, tile_values, slot_index, slot_count):
    full_panel = lax.all_gather(layer_input, "col", axis=0, tiled=True)
    partial_value = combine(tile_values, slot_index, slot_count, full_panel, True)
    return lax.psum_scatter(partial_value, "row", scatter_dimension=0, tiled=True)


def tiled_local(features, w_first, w_second, block_index, block_count, block_values, cotangent):
    slot_index = block_index[0, 0]
    slot_count = block_count[0, 0]
    tile_values = block_values[0, 0]
    feat_width = features.shape[1]
    first_linear = jnp.dot(features, w_first, preferred_element_type=jnp.float32).astype(
        jnp.bfloat16
    )
    joined = jnp.concatenate([first_linear, cotangent], axis=1)
    summed = spread_cols(joined, tile_values, slot_index, slot_count)
    first_sum = summed[:, :feat_width]
    back_second = summed[:, feat_width:].astype(jnp.bfloat16)
    first_value, act_back = jax.vjp(activate, first_sum)
    first_active = first_value.astype(jnp.bfloat16)
    second_linear = jnp.dot(first_active, w_second, preferred_element_type=jnp.float32).astype(
        jnp.bfloat16
    )
    out_second = spread_rows(second_linear, tile_values, slot_index, slot_count).astype(
        jnp.bfloat16
    )
    second_terms = jnp.einsum(
        "nf,ng->fg", first_active, back_second, preferred_element_type=jnp.float32
    )
    back_act = jnp.einsum("ng,fg->nf", back_second, w_second, preferred_element_type=jnp.float32)
    back_first = act_back(back_act)[0].astype(jnp.bfloat16)
    back_linear = spread_rows(back_first, tile_values, slot_index, slot_count).astype(jnp.bfloat16)
    first_terms = jnp.einsum("nf,ng->fg", features, back_linear, preferred_element_type=jnp.float32)
    grad_first, grad_second = lax.psum((first_terms, second_terms), ("row", "col"))
    return (out_second, grad_first, grad_second)


VMEM_SPEC = pl.BlockSpec(memory_space=pltpu.VMEM)
VMEM_LIMIT = 12 * 1024 * 1024
SMALL_LIMIT = 2 * 1024 * 1024


class Sizes:
    def __init__(self, mesh, features, block_values):
        self.n_row, self.n_col = mesh.shape["row"], mesh.shape["col"]
        self.n_dev = self.n_row * self.n_col
        self.rows, self.width = features.shape[0] // self.n_dev, features.shape[1]
        self.slots, self.block = block_values.shape[2], block_values.shape[-1]
        self.live = self.slots // 4
        self.nodes = features.shape[0]
        self.blk_rows = self.nodes // self.n_row // self.block
        self.blk_cols = self.nodes // self.n_col // self.block
        self.chunks = self.width // self.block
        self.part = self.chunks * self.rows
        self.at_cot = self.part
        self.at_val = 2 * self.part
        self.at_info = self.at_val + self.live * self.block
        self.payload = self.at_info + 16
        self.n_blocks = self.nodes // self.block

    def replicates(self):
        whole = self.n_dev * self.payload * self.block * 2
        return (
            whole <= REPLICATE_BYTES
            and self.n_col == 4
            and self.n_row % 2 == 0
            and self.n_row & (self.n_row - 1) == 0
            and 2 * self.rows == self.block
            and self.blk_rows == 2
            and self.n_blocks % 2 == 0
        )


def pack_kernel(sz, index_ref, count_ref, feat_ref, cot_ref, val_ref, out_ref, sems):
    copies = []
    for k in range(sz.chunks):
        lanes = pl.ds(k * sz.block, sz.block)
        copies.append((feat_ref.at[:, lanes], k * sz.rows, sz.rows))
        copies.append((cot_ref.at[:, lanes], sz.at_cot + k * sz.rows, sz.rows))
    for s in range(sz.live):
        copies.append((val_ref.at[0, 0, s], sz.at_val + s * sz.block, sz.block))
    copies = [
        pltpu.make_async_copy(src, out_ref.at[pl.ds(at, rows)], sems.at[n])
        for n, (src, at, rows) in enumerate(copies)
    ]
    for copy in copies:
        copy.start()
    lane = lax.broadcasted_iota(jnp.int32, (16, sz.block), 1)
    info = jnp.where(lane == 0, count_ref[0, 0], 0)
    for s in range(sz.live):
        info = jnp.where(lane == s + 1, index_ref[0, 0, s], info)
    out_ref[pl.ds(sz.at_info, 16), :] = info.astype(jnp.float32).astype(jnp.bfloat16)
    for copy in copies:
        copy.wait()


def pack(sz, features, block_index, block_count, block_values, cotangent):
    smem = pl.BlockSpec(memory_space=pltpu.SMEM)
    far = pl.BlockSpec(memory_space=pl.ANY)
    return pl.pallas_call(
        functools.partial(pack_kernel, sz),
        out_shape=pltpu.VMEM((sz.payload, sz.block), jnp.bfloat16),
        in_specs=[smem, smem, far, far, far],
        out_specs=VMEM_SPEC,
        scratch_shapes=[pltpu.SemaphoreType.DMA((2 * sz.chunks + sz.live,))],
        compiler_params=pltpu.CompilerParams(vmem_limit_bytes=SMALL_LIMIT),
    )(
        block_index,
        block_count,
        *(
            pltpu.with_memory_space_constraint(a, pltpu.HBM)
            for a in (features, cotangent, block_values)
        ),
    )


def hold(value, token):
    return pl.pallas_call(
        lambda value_ref, token_ref, out_ref: None,
        out_shape=pltpu.VMEM(value.shape, value.dtype),
        in_specs=[VMEM_SPEC, pl.BlockSpec(memory_space=pl.ANY)],
        out_specs=VMEM_SPEC,
        input_output_aliases={0: 0},
        compiler_params=pltpu.CompilerParams(vmem_limit_bytes=SMALL_LIMIT),
    )(pltpu.with_memory_space_constraint(value, pltpu.VMEM), token)


def collect(sz, payload):
    n_z = sz.n_row // 2

    def send(value, to):
        pairs = []
        for z in range(n_z):
            for y in range(2):
                for x in range(2):
                    for c in range(2):
                        z2, y2, x2, c2 = to(z, y, x, c)
                        src = (z * 2 + y) * 4 + x * 2 + c
                        pairs.append((src, (z2 * 2 + y2) * 4 + x2 * 2 + c2))
        return lax.ppermute(value, AXES, pairs)

    def first_way(z, y, x, c):
        return (z, y, 1 - x, c) if c == 0 else (z, 1 - y, x, c)

    def second_way(z, y, x, c):
        return (z, 1 - y, x, c) if c == 0 else (z, y, 1 - x, c)

    def sibling(z, y, x, c):
        return (z, y, x, 1 - c)

    def plane(own, token):
        one = send(own, first_way)
        if token is not None:
            two, three = hold(send(own, second_way), token), send(one, second_way)
            near = jnp.concatenate([own, one], axis=0)
            far = jnp.concatenate([two, three], axis=0)
            return near, far, send(near, sibling), send(far, sibling)
        near = jnp.concatenate([own, one], axis=0)
        far = send(near, second_way)
        return near, far, send(near, sibling), send(far, sibling)

    def flip(d):
        return lambda z, y, x, c: (z ^ d, y, x, c)

    held = {0: payload}
    low = 1
    while low < n_z:
        whole = 2 * low - 1
        arrived = send(payload, flip(whole))
        for d in list(held):
            held[whole ^ d] = arrived if d == 0 else send(arrived, flip(d))
        low *= 2
    order = sorted(held, key=lambda d: (d.bit_length(), -d))
    sums = None
    for d in order:
        token = sums[1] if d == order[-1] else None
        sums = add_plane(sz, plane(held[d], token), sums)
    return sums


def place():
    row, col = lax.axis_index("row"), lax.axis_index("col")
    return row // 2, row % 2, col // 2, col % 2


def plane_kernel(sz, first, *refs):
    parts, refs = refs[:4], refs[4:]
    if first:
        sums, info_v, vals_out = refs[:3]
    else:
        sums, info_v = refs[1:3]
    buf, info_s, turned, sem = refs[3:]
    _, _, x, c = place()
    block, size = sz.block, sz.payload

    for mine in range(2):

        @pl.when(c == mine)
        def _():
            for q in range(2):
                for n in range(4):
                    core = mine if q == 0 else 1 - mine
                    m = n if core == 0 else (n // 2) + 2 * (n % 2)
                    buf[m, core] = parts[2 * q + n // 2][pl.ds((n % 2) * size, size), :]

    line = lax.broadcasted_iota(jnp.int32, (8, block), 0)
    info = jnp.zeros((8, block), jnp.int32)
    for m in range(4):
        for e in range(2):
            rows = buf[m, e, pl.ds(sz.at_info, 16), :].astype(jnp.float32).astype(jnp.int32)
            info = jnp.where(line == 2 * m + e, rows[0:8], info)
    info_v[...] = info
    info_copy = pltpu.make_async_copy(info_v, info_s, sem)
    info_copy.start()

    if first:
        sums[...] = jnp.zeros_like(sums)
        for m in range(2):
            for e in range(2):
                vals_out[2 * m + e] = buf[m, e, pl.ds(sz.at_val, sz.live * block), :]

    for m in range(4):
        dx, dy = m % 2, m // 2
        for k in range(2 * sz.chunks):
            at = pl.ds(k * sz.rows, sz.rows)
            piece = jnp.concatenate([buf[m, 0, at, :], buf[m, 1, at, :]], axis=0)
            turned[2 * dy + (x ^ dx), pl.ds(k * block, block), :] = jnp.transpose(piece)
    info_copy.wait()

    for m in range(4):
        dx, dy = m % 2, m // 2
        for e in range(2):
            j = (x ^ dx) * 2 + e
            count = info_s[2 * m + e, 0]
            for s in range(sz.live):
                p = info_s[2 * m + e, s + 1]

                @pl.when(s < count)
                def _():
                    r, cb = p // sz.blk_cols, lax.rem(p, sz.blk_cols)
                    value = buf[m, e, pl.ds(sz.at_val + s * block, block), :]
                    sums[j * sz.blk_cols + cb] += jnp.dot(
                        turned[2 * dy + r], value, preferred_element_type=jnp.float32
                    )


def dense_kernel(
    sz, sums, vals, info_v, w1_ref, w2_ref, out_ref, gf_ref, gs_ref, act, w1t, rows_out, info_s, sem
):
    block, width = sz.block, sz.width
    _, _, x, c = place()
    info_copy = pltpu.make_async_copy(info_v, info_s, sem)
    info_copy.start()
    w1t[...] = jnp.transpose(w1_ref[...])
    nt = (((1,), (1,)), ((), ()))

    def chunk(n, carry):
        both = jnp.concatenate(
            [sums[2 * n].astype(jnp.bfloat16), sums[2 * n + 1].astype(jnp.bfloat16)], axis=1
        )
        g, b = both[:width], both[width:]
        v = jnp.dot(w1t[...], g, preferred_element_type=jnp.float32)
        sq = v * v
        t = jnp.tanh(GELU_C * (v + GELU_A * sq * v))
        half = 0.5 * (1.0 + t)
        a = (v * half).astype(jnp.bfloat16)
        slope = half + 0.5 * v * (1.0 - t * t) * (GELU_C * (1.0 + 3.0 * GELU_A * sq))
        act[2 * n] = a[:, :block]
        act[2 * n + 1] = a[:, block:]
        back = jnp.dot(w2_ref[...], b, preferred_element_type=jnp.float32)
        bf = (back * slope).astype(jnp.bfloat16)
        gs = lax.dot_general(a, b, nt, preferred_element_type=jnp.float32)
        gf = lax.dot_general(g, bf, nt, preferred_element_type=jnp.float32)

        @pl.when(n == 0)
        def _():
            gs_ref[...] = gs
            gf_ref[...] = gf

        @pl.when(n > 0)
        def _():
            gs_ref[...] += gs
            gf_ref[...] += gf

        return carry

    lax.fori_loop(0, sz.n_blocks // 2, chunk, 0)
    info_copy.wait()

    rows_out[...] = jnp.zeros_like(rows_out)
    for dx in range(2):
        for e in range(2):
            q = 2 * dx + e
            count = info_s[q, 0]
            for s in range(sz.live):
                p = info_s[q, s + 1]

                @pl.when((s < count) & (p // sz.blk_cols == x))
                def _():
                    cb = ((x ^ dx) * 2 + e) * sz.blk_cols + lax.rem(p, sz.blk_cols)
                    rows_out[...] += lax.dot_general(
                        act[cb],
                        vals[q, pl.ds(s * block, block), :],
                        nt,
                        preferred_element_type=jnp.float32,
                    )

    h = jnp.transpose(rows_out[...])
    high = h.astype(jnp.bfloat16)
    low = (h - high.astype(jnp.float32)).astype(jnp.bfloat16)
    out = jnp.dot(high, w2_ref[...], preferred_element_type=jnp.float32)
    out += jnp.dot(low, w2_ref[...], preferred_element_type=jnp.float32)
    out = jnp.where(c == 0, out[: sz.rows], out[sz.rows :])
    out_ref[...] = out.astype(jnp.bfloat16)


def add_plane(sz, parts, sums):
    parts = [pltpu.with_memory_space_constraint(a, pltpu.VMEM) for a in parts]
    sums_type = pltpu.VMEM((sz.n_blocks, 2 * sz.width, sz.block), jnp.float32)
    token_type = pltpu.VMEM((8, sz.block), jnp.int32)
    params = dict(
        scratch_shapes=[
            pltpu.VMEM((4, 2, sz.payload, sz.block), jnp.bfloat16),
            pltpu.SMEM((8, sz.block), jnp.int32),
            pltpu.VMEM((4, 2 * sz.width, sz.block), jnp.bfloat16),
            pltpu.SemaphoreType.DMA,
        ],
        compiler_params=pltpu.CompilerParams(vmem_limit_bytes=VMEM_LIMIT),
    )
    if sums is None:
        vals_type = pltpu.VMEM((4, sz.live * sz.block, sz.block), jnp.bfloat16)
        total, token, vals = pl.pallas_call(
            functools.partial(plane_kernel, sz, True),
            out_shape=(sums_type, token_type, vals_type),
            in_specs=[VMEM_SPEC] * 4,
            out_specs=[VMEM_SPEC] * 3,
            **params,
        )(*parts)
        return total, token, vals, token
    total, token = pl.pallas_call(
        functools.partial(plane_kernel, sz, False),
        out_shape=(sums_type, token_type),
        in_specs=[VMEM_SPEC] * 5,
        out_specs=[VMEM_SPEC] * 2,
        input_output_aliases={4: 0},
        **params,
    )(*parts, pltpu.with_memory_space_constraint(sums[0], pltpu.VMEM))
    return total, token, *sums[2:]


def dense(sz, sums, vals, info, w_first, w_second):
    grad = jax.ShapeDtypeStruct((sz.width, sz.width), jnp.float32)
    inputs = [pltpu.with_memory_space_constraint(a, pltpu.VMEM) for a in (sums, vals, info)]
    return tuple(
        pl.pallas_call(
            functools.partial(dense_kernel, sz),
            out_shape=(jax.ShapeDtypeStruct((sz.rows, sz.width), jnp.bfloat16), grad, grad),
            in_specs=[VMEM_SPEC] * 5,
            out_specs=[VMEM_SPEC] * 3,
            scratch_shapes=[
                pltpu.VMEM((sz.n_blocks, sz.width, sz.block), jnp.bfloat16),
                pltpu.VMEM((sz.width, sz.width), jnp.bfloat16),
                pltpu.VMEM((sz.width, sz.block), jnp.float32),
                pltpu.SMEM((8, sz.block), jnp.int32),
                pltpu.SemaphoreType.DMA,
            ],
            compiler_params=pltpu.CompilerParams(vmem_limit_bytes=VMEM_LIMIT),
        )(*inputs, w_first, w_second)
    )


def replicated_local(sz, features, w_first, w_second, block_index, block_count, block_values, cotangent):
    payload = pack(sz, features, block_index, block_count, block_values, cotangent)
    sums, _, vals, info = collect(sz, payload)
    return dense(sz, sums, vals, info, w_first, w_second)


def solution(mesh):
    specs = dict(
        mesh=mesh,
        in_specs=(
            P(("row", "col"), None),
            P(),
            P(),
            P("row", "col", None),
            P("row", "col"),
            P("row", "col", None, None, None),
            P(("row", "col"), None),
        ),
        out_specs=(P(("row", "col"), None), P(), P()),
        check_vma=False,
    )

    def run(features, w_first, w_second, block_index, block_count, block_values, cotangent):
        sz = Sizes(mesh, features, block_values)
        local = functools.partial(replicated_local, sz) if sz.replicates() else tiled_local
        return jax.shard_map(local, **specs)(
            features, w_first, w_second, block_index, block_count, block_values, cotangent
        )

    return run
```

```python
import functools
import math

import jax
import jax.numpy as jnp
from jax import lax
from jax.experimental import pallas as pl
from jax.experimental.pallas import tpu as pltpu
from jax.sharding import PartitionSpec as P

AXES = ("row", "col")
GELU_C = 0.7978845608028654
GELU_A = 0.044715
REPLICATE_BYTES = 8 * 1024 * 1024


def activate(v):
    return jax.nn.gelu(v, approximate=True)


def combine(tile_values, slot_index, slot_count, full_panel, flip):
    slots = slot_index.shape[0]
    block_size = tile_values.shape[-1]
    feat_width = full_panel.shape[1]
    in_blocks = full_panel.shape[0] // block_size
    if flip:
        col_blocks = slots // in_blocks
        out_blocks = col_blocks
    else:
        col_blocks = in_blocks
        out_blocks = slots // in_blocks
    group_size = math.gcd(slots, 32)
    panel_blocks = full_panel.reshape(in_blocks, block_size, feat_width)
    targets = jnp.arange(out_blocks, dtype=jnp.int32)
    offsets = jnp.arange(group_size, dtype=jnp.int32)

    def add_group(group_no, total):
        first_slot = group_no * group_size
        slot_ids = lax.dynamic_slice_in_dim(slot_index, first_slot, group_size, 0)
        group_values = lax.dynamic_slice_in_dim(tile_values, first_slot, group_size, 0)
        block_row = slot_ids // col_blocks
        block_col = slot_ids % col_blocks
        if flip:
            picked = panel_blocks[block_row]
            product = jnp.einsum(
                "sab,saf->sbf", group_values, picked, preferred_element_type=jnp.float32
            )
            target = block_col
        else:
            picked = panel_blocks[block_col]
            product = jnp.einsum(
                "sab,sbf->saf", group_values, picked, preferred_element_type=jnp.float32
            )
            target = block_row
        is_live = first_slot + offsets < slot_count
        onehot = ((target[None, :] == targets[:, None]) & is_live[None, :]).astype(jnp.float32)
        return total + jnp.einsum("os,saf->oaf", onehot, product, precision=lax.Precision.HIGHEST)

    groups = (slot_count + group_size - 1) // group_size
    total = lax.fori_loop(
        0, groups, add_group, jnp.zeros((out_blocks, block_size, feat_width), jnp.float32)
    )
    return total.reshape(out_blocks * block_size, feat_width)


def spread_rows(layer_input, tile_values, slot_index, slot_count):
    full_panel = lax.all_gather(layer_input, "row", axis=0, tiled=True)
    partial_value = combine(tile_values, slot_index, slot_count, full_panel, False)
    return lax.psum_scatter(partial_value, "col", scatter_dimension=0, tiled=True)


def spread_cols(layer_input, tile_values, slot_index, slot_count):
    full_panel = lax.all_gather(layer_input, "col", axis=0, tiled=True)
    partial_value = combine(tile_values, slot_index, slot_count, full_panel, True)
    return lax.psum_scatter(partial_value, "row", scatter_dimension=0, tiled=True)


def tiled_local(features, w_first, w_second, block_index, block_count, block_values, cotangent):
    slot_index = block_index[0, 0]
    slot_count = block_count[0, 0]
    tile_values = block_values[0, 0]
    feat_width = features.shape[1]
    first_linear = jnp.dot(features, w_first, preferred_element_type=jnp.float32).astype(
        jnp.bfloat16
    )
    joined = jnp.concatenate([first_linear, cotangent], axis=1)
    summed = spread_cols(joined, tile_values, slot_index, slot_count)
    first_sum = summed[:, :feat_width]
    back_second = summed[:, feat_width:].astype(jnp.bfloat16)
    first_value, act_back = jax.vjp(activate, first_sum)
    first_active = first_value.astype(jnp.bfloat16)
    second_linear = jnp.dot(first_active, w_second, preferred_element_type=jnp.float32).astype(
        jnp.bfloat16
    )
    out_second = spread_rows(second_linear, tile_values, slot_index, slot_count).astype(
        jnp.bfloat16
    )
    second_terms = jnp.einsum(
        "nf,ng->fg", first_active, back_second, preferred_element_type=jnp.float32
    )
    back_act = jnp.einsum("ng,fg->nf", back_second, w_second, preferred_element_type=jnp.float32)
    back_first = act_back(back_act)[0].astype(jnp.bfloat16)
    back_linear = spread_rows(back_first, tile_values, slot_index, slot_count).astype(jnp.bfloat16)
    first_terms = jnp.einsum("nf,ng->fg", features, back_linear, preferred_element_type=jnp.float32)
    grad_first, grad_second = lax.psum((first_terms, second_terms), ("row", "col"))
    return (out_second, grad_first, grad_second)


VMEM_SPEC = pl.BlockSpec(memory_space=pltpu.VMEM)
VMEM_LIMIT = 12 * 1024 * 1024
DENSE_LIMIT = 20 * 1024 * 1024
SMALL_LIMIT = 2 * 1024 * 1024


class Sizes:
    def __init__(self, mesh, features, block_values):
        self.n_row, self.n_col = mesh.shape["row"], mesh.shape["col"]
        self.n_dev = self.n_row * self.n_col
        self.rows, self.width = features.shape[0] // self.n_dev, features.shape[1]
        self.slots, self.block = block_values.shape[2], block_values.shape[-1]
        self.live = self.slots // 4
        self.nodes = features.shape[0]
        self.blk_rows = self.nodes // self.n_row // self.block
        self.blk_cols = self.nodes // self.n_col // self.block
        self.chunks = self.width // self.block
        self.part = self.chunks * self.rows
        self.at_cot = self.part
        self.at_val = 2 * self.part
        self.at_info = self.at_val + self.live * self.block
        self.payload = self.at_info + 16
        self.n_blocks = self.nodes // self.block

    def replicates(self):
        whole = self.n_dev * self.payload * self.block * 2
        return (
            whole <= REPLICATE_BYTES
            and self.n_col == 4
            and self.n_row % 2 == 0
            and self.n_row & (self.n_row - 1) == 0
            and self.n_row >= 4
            and 2 * self.rows == self.block
            and self.blk_rows == 2
            and self.n_blocks % 2 == 0
        )


def pack_kernel(sz, index_ref, count_ref, feat_ref, cot_ref, val_ref, out_ref, sems):
    copies = []
    for k in range(sz.chunks):
        lanes = pl.ds(k * sz.block, sz.block)
        copies.append((feat_ref.at[:, lanes], k * sz.rows, sz.rows))
        copies.append((cot_ref.at[:, lanes], sz.at_cot + k * sz.rows, sz.rows))
    for s in range(sz.live):
        copies.append((val_ref.at[0, 0, s], sz.at_val + s * sz.block, sz.block))
    copies = [
        pltpu.make_async_copy(src, out_ref.at[pl.ds(at, rows)], sems.at[n])
        for n, (src, at, rows) in enumerate(copies)
    ]
    for copy in copies:
        copy.start()
    lane = lax.broadcasted_iota(jnp.int32, (16, sz.block), 1)
    info = jnp.where(lane == 0, count_ref[0, 0], 0)
    for s in range(sz.live):
        info = jnp.where(lane == s + 1, index_ref[0, 0, s], info)
    out_ref[pl.ds(sz.at_info, 16), :] = info.astype(jnp.float32).astype(jnp.bfloat16)
    for copy in copies:
        copy.wait()


def pack(sz, features, block_index, block_count, block_values, cotangent):
    smem = pl.BlockSpec(memory_space=pltpu.SMEM)
    far = pl.BlockSpec(memory_space=pl.ANY)
    return pl.pallas_call(
        functools.partial(pack_kernel, sz),
        out_shape=pltpu.VMEM((sz.payload, sz.block), jnp.bfloat16),
        in_specs=[smem, smem, far, far, far],
        out_specs=VMEM_SPEC,
        scratch_shapes=[pltpu.SemaphoreType.DMA((2 * sz.chunks + sz.live,))],
        compiler_params=pltpu.CompilerParams(vmem_limit_bytes=SMALL_LIMIT),
    )(
        block_index,
        block_count,
        *(
            pltpu.with_memory_space_constraint(a, pltpu.HBM)
            for a in (features, cotangent, block_values)
        ),
    )


def hold(value, token):
    return pl.pallas_call(
        lambda value_ref, token_ref, out_ref: None,
        out_shape=pltpu.VMEM(value.shape, value.dtype),
        in_specs=[VMEM_SPEC, pl.BlockSpec(memory_space=pl.ANY)],
        out_specs=VMEM_SPEC,
        input_output_aliases={0: 0},
        compiler_params=pltpu.CompilerParams(vmem_limit_bytes=SMALL_LIMIT),
    )(pltpu.with_memory_space_constraint(value, pltpu.VMEM), token)


def collect(sz, payload, w_first):
    n_z = sz.n_row // 2

    def send(value, to):
        pairs = []
        for z in range(n_z):
            for y in range(2):
                for x in range(2):
                    for c in range(2):
                        z2, y2, x2, c2 = to(z, y, x, c)
                        src = (z * 2 + y) * 4 + x * 2 + c
                        pairs.append((src, (z2 * 2 + y2) * 4 + x2 * 2 + c2))
        return lax.ppermute(value, AXES, pairs)

    def first_way(z, y, x, c):
        return (z, y, 1 - x, c) if c == 0 else (z, 1 - y, x, c)

    def second_way(z, y, x, c):
        return (z, 1 - y, x, c) if c == 0 else (z, y, 1 - x, c)

    def sibling(z, y, x, c):
        return (z, y, x, 1 - c)

    def flip(d):
        return lambda z, y, x, c: (z ^ d, y, x, c)

    def pair(a, b):
        return jnp.concatenate([a, b], axis=0)

    def plane(near, far):
        return near, far, send(near, sibling), send(far, sibling)

    one = send(payload, first_way)
    near = pair(payload, one)
    planes = [(near, send(near, second_way))]
    near = send(near, flip(1))
    planes.append((near, send(near, second_way)))
    sums, token, w1t = init(sz, w_first, one)

    low = 2
    while low < n_z:
        own = hold(send(payload, flip(2 * low - 1)), token)
        one = send(own, first_way)
        near = pair(own, one)
        planes.append((near, pair(send(own, second_way), send(one, second_way))))
        for d in range(1, low):
            passed = send(near, flip(d))
            planes.append((passed, send(passed, second_way)))
        low *= 2

    sums, info, vals = add_plane(sz, plane(*planes[0]), sums, True)
    token = info
    for near, far in planes[1:-1]:
        sums, token = add_plane(sz, plane(near, far), sums, False)
    near, far = planes[-1]
    sums, token = add_plane(sz, plane(near, hold(far, token)), sums, False)
    return sums, vals, info, w1t


def place():
    row, col = lax.axis_index("row"), lax.axis_index("col")
    return row // 2, row % 2, col // 2, col % 2


def plane_kernel(sz, first, *refs):
    parts, refs = refs[:4], refs[4:]
    sums, info_v = refs[1:3]
    vals_out = refs[3] if first else None
    buf, info_s, turned, sem = refs[-4:]
    _, _, x, c = place()
    block, size = sz.block, sz.payload

    for mine in range(2):

        @pl.when(c == mine)
        def _():
            for q in range(2):
                for n in range(4):
                    core = mine if q == 0 else 1 - mine
                    m = n if core == 0 else (n // 2) + 2 * (n % 2)
                    buf[m, core] = parts[2 * q + n // 2][pl.ds((n % 2) * size, size), :]

    line = lax.broadcasted_iota(jnp.int32, (8, block), 0)
    info = jnp.zeros((8, block), jnp.int32)
    for m in range(4):
        for e in range(2):
            rows = buf[m, e, pl.ds(sz.at_info, 16), :].astype(jnp.float32).astype(jnp.int32)
            info = jnp.where(line == 2 * m + e, rows[0:8], info)
    info_v[...] = info
    info_copy = pltpu.make_async_copy(info_v, info_s, sem)
    info_copy.start()

    if first:
        for m in range(2):
            for e in range(2):
                vals_out[2 * m + e] = buf[m, e, pl.ds(sz.at_val, sz.live * block), :]

    for m in range(4):
        dx, dy = m % 2, m // 2
        for k in range(2 * sz.chunks):
            at = pl.ds(k * sz.rows, sz.rows)
            piece = jnp.concatenate([buf[m, 0, at, :], buf[m, 1, at, :]], axis=0)
            turned[2 * dy + (x ^ dx), pl.ds(k * block, block), :] = jnp.transpose(piece)
    info_copy.wait()

    for m in range(4):
        dx, dy = m % 2, m // 2
        for e in range(2):
            j = (x ^ dx) * 2 + e
            count = info_s[2 * m + e, 0]
            for s in range(sz.live):
                p = info_s[2 * m + e, s + 1]

                @pl.when(s < count)
                def _():
                    r, cb = p // sz.blk_cols, lax.rem(p, sz.blk_cols)
                    value = buf[m, e, pl.ds(sz.at_val + s * block, block), :]
                    sums[j * sz.blk_cols + cb] += jnp.dot(
                        turned[2 * dy + r], value, preferred_element_type=jnp.float32
                    )


def dense_kernel(
    sz, sums, vals, info_v, w1t, w2_ref, out_ref, gf_ref, gs_ref, act, rows_out, info_s, sems, *wide
):
    block, width = sz.block, sz.width
    _, _, x, c = place()
    info_copy = pltpu.make_async_copy(info_v, info_s, sems.at[0])
    info_copy.start()
    nt = (((1,), (1,)), ((), ()))
    all_g, all_b, all_a, all_f, gs, gf = wide

    for n in range(sz.n_blocks // 2):
        lanes = pl.ds(2 * n * block, 2 * block)
        both = jnp.concatenate(
            [sums[2 * n].astype(jnp.bfloat16), sums[2 * n + 1].astype(jnp.bfloat16)], axis=1
        )
        g, b = both[:width], both[width:]
        all_g[:, lanes] = g
        all_b[:, lanes] = b
        v = jnp.dot(w1t[...], g, preferred_element_type=jnp.float32)
        sq = v * v
        t = jnp.tanh(GELU_C * (v + GELU_A * sq * v))
        half = 0.5 * (1.0 + t)
        a = (v * half).astype(jnp.bfloat16)
        slope = half + 0.5 * v * (1.0 - t * t) * (GELU_C * (1.0 + 3.0 * GELU_A * sq))
        act[2 * n] = a[:, :block]
        act[2 * n + 1] = a[:, block:]
        all_a[:, lanes] = a
        back = jnp.dot(w2_ref[...], b, preferred_element_type=jnp.float32)
        all_f[:, lanes] = (back * slope).astype(jnp.bfloat16)

    gs[...] = lax.dot_general(all_a[...], all_b[...], nt, preferred_element_type=jnp.float32)
    gs_copy = pltpu.make_async_copy(gs, gs_ref, sems.at[1])
    gs_copy.start()
    gf[...] = lax.dot_general(all_g[...], all_f[...], nt, preferred_element_type=jnp.float32)
    gf_copy = pltpu.make_async_copy(gf, gf_ref, sems.at[2])
    gf_copy.start()
    info_copy.wait()

    rows_out[...] = jnp.zeros_like(rows_out)
    for dx in range(2):
        for e in range(2):
            q = 2 * dx + e
            count = info_s[q, 0]
            for s in range(sz.live):
                p = info_s[q, s + 1]

                @pl.when((s < count) & (p // sz.blk_cols == x))
                def _():
                    cb = ((x ^ dx) * 2 + e) * sz.blk_cols + lax.rem(p, sz.blk_cols)
                    rows_out[...] += lax.dot_general(
                        act[cb],
                        vals[q, pl.ds(s * block, block), :],
                        nt,
                        preferred_element_type=jnp.float32,
                    )

    h = jnp.transpose(rows_out[...])
    high = h.astype(jnp.bfloat16)
    low = (h - high.astype(jnp.float32)).astype(jnp.bfloat16)
    out = jnp.dot(high, w2_ref[...], preferred_element_type=jnp.float32)
    out += jnp.dot(low, w2_ref[...], preferred_element_type=jnp.float32)
    out = jnp.where(c == 0, out[: sz.rows], out[sz.rows :])
    out_ref[...] = out.astype(jnp.bfloat16)
    gs_copy.wait()
    gf_copy.wait()


def init_kernel(w1_ref, dep_ref, sums, token, w1t):
    sums[...] = jnp.zeros_like(sums)
    token[...] = jnp.zeros_like(token)
    w1t[...] = jnp.transpose(w1_ref[...])


def init(sz, w_first, dep):
    return pl.pallas_call(
        init_kernel,
        out_shape=(
            pltpu.VMEM((sz.n_blocks, 2 * sz.width, sz.block), jnp.float32),
            pltpu.VMEM((8, sz.block), jnp.int32),
            pltpu.VMEM((sz.width, sz.width), jnp.bfloat16),
        ),
        in_specs=[VMEM_SPEC, pl.BlockSpec(memory_space=pl.ANY)],
        out_specs=[VMEM_SPEC] * 3,
        compiler_params=pltpu.CompilerParams(vmem_limit_bytes=SMALL_LIMIT),
    )(w_first, dep)


def add_plane(sz, parts, sums, first):
    parts = [pltpu.with_memory_space_constraint(a, pltpu.VMEM) for a in (*parts, sums)]
    out_shape = [
        pltpu.VMEM((sz.n_blocks, 2 * sz.width, sz.block), jnp.float32),
        pltpu.VMEM((8, sz.block), jnp.int32),
    ]
    if first:
        out_shape.append(pltpu.VMEM((4, sz.live * sz.block, sz.block), jnp.bfloat16))
    return pl.pallas_call(
        functools.partial(plane_kernel, sz, first),
        out_shape=tuple(out_shape),
        in_specs=[VMEM_SPEC] * 5,
        out_specs=[VMEM_SPEC] * len(out_shape),
        input_output_aliases={4: 0},
        scratch_shapes=[
            pltpu.VMEM((4, 2, sz.payload, sz.block), jnp.bfloat16),
            pltpu.SMEM((8, sz.block), jnp.int32),
            pltpu.VMEM((4, 2 * sz.width, sz.block), jnp.bfloat16),
            pltpu.SemaphoreType.DMA,
        ],
        compiler_params=pltpu.CompilerParams(vmem_limit_bytes=VMEM_LIMIT),
    )(*parts)


def dense(sz, sums, vals, info, w1t, w_second):
    grad = jax.ShapeDtypeStruct((sz.width, sz.width), jnp.float32)
    inputs = [pltpu.with_memory_space_constraint(a, pltpu.VMEM) for a in (sums, vals, info, w1t)]
    far = pl.BlockSpec(memory_space=pl.ANY)
    return tuple(
        pl.pallas_call(
            functools.partial(dense_kernel, sz),
            out_shape=(jax.ShapeDtypeStruct((sz.rows, sz.width), jnp.bfloat16), grad, grad),
            in_specs=[VMEM_SPEC] * 5,
            out_specs=[VMEM_SPEC, far, far],
            scratch_shapes=[
                pltpu.VMEM((sz.n_blocks, sz.width, sz.block), jnp.bfloat16),
                pltpu.VMEM((sz.width, sz.block), jnp.float32),
                pltpu.SMEM((8, sz.block), jnp.int32),
                pltpu.SemaphoreType.DMA((3,)),
            ]
            + [pltpu.VMEM((sz.width, sz.nodes), jnp.bfloat16)] * 4
            + [pltpu.VMEM((sz.width, sz.width), jnp.float32)] * 2,
            compiler_params=pltpu.CompilerParams(vmem_limit_bytes=DENSE_LIMIT),
        )(*inputs, w_second)
    )


def replicated_local(sz, features, w_first, w_second, block_index, block_count, block_values, cotangent):
    payload = pack(sz, features, block_index, block_count, block_values, cotangent)
    sums, vals, info, w1t = collect(sz, payload, w_first)
    return dense(sz, sums, vals, info, w1t, w_second)


def solution(mesh):
    specs = dict(
        mesh=mesh,
        in_specs=(
            P(("row", "col"), None),
            P(),
            P(),
            P("row", "col", None),
            P("row", "col"),
            P("row", "col", None, None, None),
            P(("row", "col"), None),
        ),
        out_specs=(P(("row", "col"), None), P(), P()),
        check_vma=False,
    )

    def run(features, w_first, w_second, block_index, block_count, block_values, cotangent):
        sz = Sizes(mesh, features, block_values)
        local = functools.partial(replicated_local, sz) if sz.replicates() else tiled_local
        return jax.shard_map(local, **specs)(
            features, w_first, w_second, block_index, block_count, block_values, cotangent
        )

    return run
```

```python
import functools
import math

import jax
import jax.numpy as jnp
from jax import lax
from jax.experimental import pallas as pl
from jax.experimental.pallas import tpu as pltpu
from jax.sharding import PartitionSpec as P

AXES = ("row", "col")
GELU_C = 0.7978845608028654
GELU_A = 0.044715
REPLICATE_BYTES = 8 * 1024 * 1024


def activate(v):
    return jax.nn.gelu(v, approximate=True)


def combine(tile_values, slot_index, slot_count, full_panel, flip):
    slots = slot_index.shape[0]
    block_size = tile_values.shape[-1]
    feat_width = full_panel.shape[1]
    in_blocks = full_panel.shape[0] // block_size
    if flip:
        col_blocks = slots // in_blocks
        out_blocks = col_blocks
    else:
        col_blocks = in_blocks
        out_blocks = slots // in_blocks
    group_size = math.gcd(slots, 32)
    panel_blocks = full_panel.reshape(in_blocks, block_size, feat_width)
    targets = jnp.arange(out_blocks, dtype=jnp.int32)
    offsets = jnp.arange(group_size, dtype=jnp.int32)

    def add_group(group_no, total):
        first_slot = group_no * group_size
        slot_ids = lax.dynamic_slice_in_dim(slot_index, first_slot, group_size, 0)
        group_values = lax.dynamic_slice_in_dim(tile_values, first_slot, group_size, 0)
        block_row = slot_ids // col_blocks
        block_col = slot_ids % col_blocks
        if flip:
            picked = panel_blocks[block_row]
            product = jnp.einsum(
                "sab,saf->sbf", group_values, picked, preferred_element_type=jnp.float32
            )
            target = block_col
        else:
            picked = panel_blocks[block_col]
            product = jnp.einsum(
                "sab,sbf->saf", group_values, picked, preferred_element_type=jnp.float32
            )
            target = block_row
        is_live = first_slot + offsets < slot_count
        onehot = ((target[None, :] == targets[:, None]) & is_live[None, :]).astype(jnp.float32)
        return total + jnp.einsum("os,saf->oaf", onehot, product, precision=lax.Precision.HIGHEST)

    groups = (slot_count + group_size - 1) // group_size
    total = lax.fori_loop(
        0, groups, add_group, jnp.zeros((out_blocks, block_size, feat_width), jnp.float32)
    )
    return total.reshape(out_blocks * block_size, feat_width)


def spread_rows(layer_input, tile_values, slot_index, slot_count):
    full_panel = lax.all_gather(layer_input, "row", axis=0, tiled=True)
    partial_value = combine(tile_values, slot_index, slot_count, full_panel, False)
    return lax.psum_scatter(partial_value, "col", scatter_dimension=0, tiled=True)


def spread_cols(layer_input, tile_values, slot_index, slot_count):
    full_panel = lax.all_gather(layer_input, "col", axis=0, tiled=True)
    partial_value = combine(tile_values, slot_index, slot_count, full_panel, True)
    return lax.psum_scatter(partial_value, "row", scatter_dimension=0, tiled=True)


def tiled_local(features, w_first, w_second, block_index, block_count, block_values, cotangent):
    slot_index = block_index[0, 0]
    slot_count = block_count[0, 0]
    tile_values = block_values[0, 0]
    feat_width = features.shape[1]
    first_linear = jnp.dot(features, w_first, preferred_element_type=jnp.float32).astype(
        jnp.bfloat16
    )
    joined = jnp.concatenate([first_linear, cotangent], axis=1)
    summed = spread_cols(joined, tile_values, slot_index, slot_count)
    first_sum = summed[:, :feat_width]
    back_second = summed[:, feat_width:].astype(jnp.bfloat16)
    first_value, act_back = jax.vjp(activate, first_sum)
    first_active = first_value.astype(jnp.bfloat16)
    second_linear = jnp.dot(first_active, w_second, preferred_element_type=jnp.float32).astype(
        jnp.bfloat16
    )
    out_second = spread_rows(second_linear, tile_values, slot_index, slot_count).astype(
        jnp.bfloat16
    )
    second_terms = jnp.einsum(
        "nf,ng->fg", first_active, back_second, preferred_element_type=jnp.float32
    )
    back_act = jnp.einsum("ng,fg->nf", back_second, w_second, preferred_element_type=jnp.float32)
    back_first = act_back(back_act)[0].astype(jnp.bfloat16)
    back_linear = spread_rows(back_first, tile_values, slot_index, slot_count).astype(jnp.bfloat16)
    first_terms = jnp.einsum("nf,ng->fg", features, back_linear, preferred_element_type=jnp.float32)
    grad_first, grad_second = lax.psum((first_terms, second_terms), ("row", "col"))
    return (out_second, grad_first, grad_second)


VMEM_SPEC = pl.BlockSpec(memory_space=pltpu.VMEM)
VMEM_LIMIT = 12 * 1024 * 1024
DENSE_LIMIT = 20 * 1024 * 1024
SMALL_LIMIT = 2 * 1024 * 1024


class Sizes:
    def __init__(self, mesh, features, block_values):
        self.n_row, self.n_col = mesh.shape["row"], mesh.shape["col"]
        self.n_dev = self.n_row * self.n_col
        self.rows, self.width = features.shape[0] // self.n_dev, features.shape[1]
        self.slots, self.block = block_values.shape[2], block_values.shape[-1]
        self.live = self.slots // 4
        self.nodes = features.shape[0]
        self.blk_rows = self.nodes // self.n_row // self.block
        self.blk_cols = self.nodes // self.n_col // self.block
        self.chunks = self.width // self.block
        self.part = self.chunks * self.rows
        self.at_cot = self.part
        self.at_val = 2 * self.part
        self.at_info = self.at_val + self.live * self.block
        self.payload = self.at_info + 16
        self.n_blocks = self.nodes // self.block

    def replicates(self):
        whole = self.n_dev * self.payload * self.block * 2
        return (
            whole <= REPLICATE_BYTES
            and self.n_col == 4
            and self.n_row % 2 == 0
            and self.n_row & (self.n_row - 1) == 0
            and self.n_row >= 4
            and 2 * self.rows == self.block
            and self.blk_rows == 2
            and self.n_blocks % 2 == 0
        )


def pack_kernel(
    sz, index_ref, count_ref, feat_ref, cot_ref, val_ref, out_ref, index_s, small_sems, sems
):
    small = [
        pltpu.make_async_copy(index_ref, index_s, small_sems.at[0]),
    ]
    for copy in small:
        copy.start()
    copies = []
    for k in range(sz.chunks):
        lanes = pl.ds(k * sz.block, sz.block)
        copies.append((feat_ref.at[:, lanes], k * sz.rows, sz.rows))
        copies.append((cot_ref.at[:, lanes], sz.at_cot + k * sz.rows, sz.rows))
    for s in range(sz.live):
        copies.append((val_ref.at[0, 0, s], sz.at_val + s * sz.block, sz.block))
    copies = [
        pltpu.make_async_copy(src, out_ref.at[pl.ds(at, rows)], sems.at[n])
        for n, (src, at, rows) in enumerate(copies)
    ]
    for copy in copies:
        copy.start()
    for copy in small:
        copy.wait()
    lane = lax.broadcasted_iota(jnp.int32, (16, sz.block), 1)
    info = jnp.where(lane == 0, count_ref[0, 0], 0)
    for s in range(sz.live):
        info = jnp.where(lane == s + 1, index_s[0, 0, s], info)
    out_ref[pl.ds(sz.at_info, 16), :] = info.astype(jnp.float32).astype(jnp.bfloat16)
    for copy in copies:
        copy.wait()


def pack(sz, features, block_index, block_count, block_values, cotangent):
    far = pl.BlockSpec(memory_space=pl.ANY)
    return pl.pallas_call(
        functools.partial(pack_kernel, sz),
        out_shape=pltpu.VMEM((sz.payload, sz.block), jnp.bfloat16),
        in_specs=[far, pl.BlockSpec(memory_space=pltpu.SMEM), far, far, far],
        out_specs=VMEM_SPEC,
        scratch_shapes=[
            pltpu.SMEM(block_index.shape, jnp.int32),
            pltpu.SemaphoreType.DMA((1,)),
            pltpu.SemaphoreType.DMA((2 * sz.chunks + sz.live,)),
        ],
        compiler_params=pltpu.CompilerParams(vmem_limit_bytes=SMALL_LIMIT),
    )(
        pltpu.with_memory_space_constraint(block_index, pltpu.HBM),
        block_count,
        *(
            pltpu.with_memory_space_constraint(a, pltpu.HBM)
            for a in (features, cotangent, block_values)
        ),
    )


def hold(value, token):
    return pl.pallas_call(
        lambda value_ref, token_ref, out_ref: None,
        out_shape=pltpu.VMEM(value.shape, value.dtype),
        in_specs=[VMEM_SPEC, pl.BlockSpec(memory_space=pl.ANY)],
        out_specs=VMEM_SPEC,
        input_output_aliases={0: 0},
        compiler_params=pltpu.CompilerParams(vmem_limit_bytes=SMALL_LIMIT),
    )(pltpu.with_memory_space_constraint(value, pltpu.VMEM), token)


def collect(sz, payload, w_first):
    n_z = sz.n_row // 2

    def send(value, to):
        pairs = []
        for z in range(n_z):
            for y in range(2):
                for x in range(2):
                    for c in range(2):
                        z2, y2, x2, c2 = to(z, y, x, c)
                        src = (z * 2 + y) * 4 + x * 2 + c
                        pairs.append((src, (z2 * 2 + y2) * 4 + x2 * 2 + c2))
        return lax.ppermute(value, AXES, pairs)

    def first_way(z, y, x, c):
        return (z, y, 1 - x, c) if c == 0 else (z, 1 - y, x, c)

    def second_way(z, y, x, c):
        return (z, 1 - y, x, c) if c == 0 else (z, y, 1 - x, c)

    def sibling(z, y, x, c):
        return (z, y, x, 1 - c)

    def flip(d):
        return lambda z, y, x, c: (z ^ d, y, x, c)

    def pair(a, b):
        return jnp.concatenate([a, b], axis=0)

    def plane(near, far):
        return near, far, send(near, sibling), send(far, sibling)

    one = send(payload, first_way)
    near = pair(payload, one)
    planes = [(near, send(near, second_way))]
    near = send(near, flip(1))
    planes.append((near, send(near, second_way)))
    sums, token, w1t = init(sz, w_first, one)

    low = 2
    while low < n_z:
        own = hold(send(payload, flip(2 * low - 1)), token)
        one = send(own, first_way)
        near = pair(own, one)
        planes.append((near, pair(send(own, second_way), send(one, second_way))))
        for d in range(1, low):
            passed = send(near, flip(d))
            planes.append((passed, send(passed, second_way)))
        low *= 2

    sums, info, vals = add_plane(sz, plane(*planes[0]), sums, True)
    token = info
    for near, far in planes[1:-1]:
        sums, token = add_plane(sz, plane(near, far), sums, False)
    near, far = planes[-1]
    sums, token = add_plane(sz, plane(near, hold(far, token)), sums, False)
    return sums, vals, info, w1t


def place():
    row, col = lax.axis_index("row"), lax.axis_index("col")
    return row // 2, row % 2, col // 2, col % 2


def plane_kernel(sz, first, *refs):
    parts, refs = refs[:4], refs[4:]
    sums, info_v = refs[1:3]
    vals_out = refs[3] if first else None
    buf, info_s, turned, sem = refs[-4:]
    _, _, x, c = place()
    block, size = sz.block, sz.payload

    for mine in range(2):

        @pl.when(c == mine)
        def _():
            for q in range(2):
                for n in range(4):
                    core = mine if q == 0 else 1 - mine
                    m = n if core == 0 else (n // 2) + 2 * (n % 2)
                    buf[m, core] = parts[2 * q + n // 2][pl.ds((n % 2) * size, size), :]

    line = lax.broadcasted_iota(jnp.int32, (8, block), 0)
    info = jnp.zeros((8, block), jnp.int32)
    for m in range(4):
        for e in range(2):
            rows = buf[m, e, pl.ds(sz.at_info, 16), :].astype(jnp.float32).astype(jnp.int32)
            info = jnp.where(line == 2 * m + e, rows[0:8], info)
    info_v[...] = info
    info_copy = pltpu.make_async_copy(info_v, info_s, sem)
    info_copy.start()

    if first:
        for m in range(2):
            for e in range(2):
                vals_out[2 * m + e] = buf[m, e, pl.ds(sz.at_val, sz.live * block), :]

    for m in range(4):
        dx, dy = m % 2, m // 2
        for k in range(2 * sz.chunks):
            at = pl.ds(k * sz.rows, sz.rows)
            piece = jnp.concatenate([buf[m, 0, at, :], buf[m, 1, at, :]], axis=0)
            turned[2 * dy + (x ^ dx), pl.ds(k * block, block), :] = jnp.transpose(piece)
    info_copy.wait()

    for m in range(4):
        dx, dy = m % 2, m // 2
        for e in range(2):
            j = (x ^ dx) * 2 + e
            count = info_s[2 * m + e, 0]
            for s in range(sz.live):
                p = info_s[2 * m + e, s + 1]

                @pl.when(s < count)
                def _():
                    r, cb = p // sz.blk_cols, lax.rem(p, sz.blk_cols)
                    value = buf[m, e, pl.ds(sz.at_val + s * block, block), :]
                    sums[j * sz.blk_cols + cb] += jnp.dot(
                        turned[2 * dy + r], value, preferred_element_type=jnp.float32
                    )


def dense_kernel(
    sz, sums, vals, info_v, w1t, w2_ref, out_ref, gf_ref, gs_ref, act, rows_out, info_s, sems, *wide
):
    block, width = sz.block, sz.width
    _, _, x, c = place()
    info_copy = pltpu.make_async_copy(info_v, info_s, sems.at[0])
    info_copy.start()
    nt = (((1,), (1,)), ((), ()))
    all_g, all_b, all_a, all_f, gs, gf = wide

    for n in range(sz.n_blocks // 2):
        lanes = pl.ds(2 * n * block, 2 * block)
        both = jnp.concatenate(
            [sums[2 * n].astype(jnp.bfloat16), sums[2 * n + 1].astype(jnp.bfloat16)], axis=1
        )
        g, b = both[:width], both[width:]
        all_g[:, lanes] = g
        all_b[:, lanes] = b
        v = jnp.dot(w1t[...], g, preferred_element_type=jnp.float32)
        p = GELU_C + (GELU_C * GELU_A) * (v * v)
        half = 0.5 + 0.5 * jnp.tanh(v * p)
        value = v * half
        slope = half + (value * (1.0 - half)) * (6.0 * p - 4.0 * GELU_C)
        a = value.astype(jnp.bfloat16)
        act[2 * n] = a[:, :block]
        act[2 * n + 1] = a[:, block:]
        all_a[:, lanes] = a
        back = jnp.dot(w2_ref[...], b, preferred_element_type=jnp.float32)
        all_f[:, lanes] = (back * slope).astype(jnp.bfloat16)

    gs[...] = lax.dot_general(all_a[...], all_b[...], nt, preferred_element_type=jnp.float32)
    gs_copy = pltpu.make_async_copy(gs, gs_ref, sems.at[1])
    gs_copy.start()
    gf[...] = lax.dot_general(all_g[...], all_f[...], nt, preferred_element_type=jnp.float32)
    gf_copy = pltpu.make_async_copy(gf, gf_ref, sems.at[2])
    gf_copy.start()
    info_copy.wait()

    rows_out[...] = jnp.zeros_like(rows_out)
    for dx in range(2):
        for e in range(2):
            q = 2 * dx + e
            count = info_s[q, 0]
            for s in range(sz.live):
                p = info_s[q, s + 1]

                @pl.when((s < count) & (p // sz.blk_cols == x))
                def _():
                    cb = ((x ^ dx) * 2 + e) * sz.blk_cols + lax.rem(p, sz.blk_cols)
                    rows_out[...] += lax.dot_general(
                        act[cb],
                        vals[q, pl.ds(s * block, block), :],
                        nt,
                        preferred_element_type=jnp.float32,
                    )

    h = jnp.transpose(rows_out[...])
    high = h.astype(jnp.bfloat16)
    low = (h - high.astype(jnp.float32)).astype(jnp.bfloat16)
    out = jnp.dot(high, w2_ref[...], preferred_element_type=jnp.float32)
    out += jnp.dot(low, w2_ref[...], preferred_element_type=jnp.float32)
    out = jnp.where(c == 0, out[: sz.rows], out[sz.rows :])
    out_ref[...] = out.astype(jnp.bfloat16)
    gs_copy.wait()
    gf_copy.wait()


def init_kernel(w1_ref, dep_ref, sums, token, w1t):
    sums[...] = jnp.zeros_like(sums)
    token[...] = jnp.zeros_like(token)
    w1t[...] = jnp.transpose(w1_ref[...])


def init(sz, w_first, dep):
    return pl.pallas_call(
        init_kernel,
        out_shape=(
            pltpu.VMEM((sz.n_blocks, 2 * sz.width, sz.block), jnp.float32),
            pltpu.VMEM((8, sz.block), jnp.int32),
            pltpu.VMEM((sz.width, sz.width), jnp.bfloat16),
        ),
        in_specs=[VMEM_SPEC, pl.BlockSpec(memory_space=pl.ANY)],
        out_specs=[VMEM_SPEC] * 3,
        compiler_params=pltpu.CompilerParams(vmem_limit_bytes=SMALL_LIMIT),
    )(w_first, dep)


def add_plane(sz, parts, sums, first):
    parts = [pltpu.with_memory_space_constraint(a, pltpu.VMEM) for a in (*parts, sums)]
    out_shape = [
        pltpu.VMEM((sz.n_blocks, 2 * sz.width, sz.block), jnp.float32),
        pltpu.VMEM((8, sz.block), jnp.int32),
    ]
    if first:
        out_shape.append(pltpu.VMEM((4, sz.live * sz.block, sz.block), jnp.bfloat16))
    return pl.pallas_call(
        functools.partial(plane_kernel, sz, first),
        out_shape=tuple(out_shape),
        in_specs=[VMEM_SPEC] * 5,
        out_specs=[VMEM_SPEC] * len(out_shape),
        input_output_aliases={4: 0},
        scratch_shapes=[
            pltpu.VMEM((4, 2, sz.payload, sz.block), jnp.bfloat16),
            pltpu.SMEM((8, sz.block), jnp.int32),
            pltpu.VMEM((4, 2 * sz.width, sz.block), jnp.bfloat16),
            pltpu.SemaphoreType.DMA,
        ],
        compiler_params=pltpu.CompilerParams(vmem_limit_bytes=VMEM_LIMIT),
    )(*parts)


def dense(sz, sums, vals, info, w1t, w_second):
    grad = jax.ShapeDtypeStruct((sz.width, sz.width), jnp.float32)
    inputs = [pltpu.with_memory_space_constraint(a, pltpu.VMEM) for a in (sums, vals, info, w1t)]
    far = pl.BlockSpec(memory_space=pl.ANY)
    return tuple(
        pl.pallas_call(
            functools.partial(dense_kernel, sz),
            out_shape=(jax.ShapeDtypeStruct((sz.rows, sz.width), jnp.bfloat16), grad, grad),
            in_specs=[VMEM_SPEC] * 5,
            out_specs=[VMEM_SPEC, far, far],
            scratch_shapes=[
                pltpu.VMEM((sz.n_blocks, sz.width, sz.block), jnp.bfloat16),
                pltpu.VMEM((sz.width, sz.block), jnp.float32),
                pltpu.SMEM((8, sz.block), jnp.int32),
                pltpu.SemaphoreType.DMA((3,)),
            ]
            + [pltpu.VMEM((sz.width, sz.nodes), jnp.bfloat16)] * 4
            + [pltpu.VMEM((sz.width, sz.width), jnp.float32)] * 2,
            compiler_params=pltpu.CompilerParams(vmem_limit_bytes=DENSE_LIMIT),
        )(*inputs, w_second)
    )


def replicated_local(sz, features, w_first, w_second, block_index, block_count, block_values, cotangent):
    payload = pack(sz, features, block_index, block_count, block_values, cotangent)
    sums, vals, info, w1t = collect(sz, payload, w_first)
    return dense(sz, sums, vals, info, w1t, w_second)


def solution(mesh):
    specs = dict(
        mesh=mesh,
        in_specs=(
            P(("row", "col"), None),
            P(),
            P(),
            P("row", "col", None),
            P("row", "col"),
            P("row", "col", None, None, None),
            P(("row", "col"), None),
        ),
        out_specs=(P(("row", "col"), None), P(), P()),
        check_vma=False,
    )

    def run(features, w_first, w_second, block_index, block_count, block_values, cotangent):
        sz = Sizes(mesh, features, block_values)
        local = functools.partial(replicated_local, sz) if sz.replicates() else tiled_local
        return jax.shard_map(local, **specs)(
            features, w_first, w_second, block_index, block_count, block_values, cotangent
        )

    return run
```

```python
import functools
import math

import jax
import jax.numpy as jnp
from jax import lax
from jax.experimental import pallas as pl
from jax.experimental.pallas import tpu as pltpu
from jax.sharding import PartitionSpec as P

AXES = ("row", "col")
GELU_C = 0.7978845608028654
GELU_A = 0.044715
REPLICATE_BYTES = 8 * 1024 * 1024


def activate(v):
    return jax.nn.gelu(v, approximate=True)


def combine(tile_values, slot_index, slot_count, full_panel, flip):
    slots = slot_index.shape[0]
    block_size = tile_values.shape[-1]
    feat_width = full_panel.shape[1]
    in_blocks = full_panel.shape[0] // block_size
    if flip:
        col_blocks = slots // in_blocks
        out_blocks = col_blocks
    else:
        col_blocks = in_blocks
        out_blocks = slots // in_blocks
    group_size = math.gcd(slots, 32)
    panel_blocks = full_panel.reshape(in_blocks, block_size, feat_width)
    targets = jnp.arange(out_blocks, dtype=jnp.int32)
    offsets = jnp.arange(group_size, dtype=jnp.int32)

    def add_group(group_no, total):
        first_slot = group_no * group_size
        slot_ids = lax.dynamic_slice_in_dim(slot_index, first_slot, group_size, 0)
        group_values = lax.dynamic_slice_in_dim(tile_values, first_slot, group_size, 0)
        block_row = slot_ids // col_blocks
        block_col = slot_ids % col_blocks
        if flip:
            picked = panel_blocks[block_row]
            product = jnp.einsum(
                "sab,saf->sbf", group_values, picked, preferred_element_type=jnp.float32
            )
            target = block_col
        else:
            picked = panel_blocks[block_col]
            product = jnp.einsum(
                "sab,sbf->saf", group_values, picked, preferred_element_type=jnp.float32
            )
            target = block_row
        is_live = first_slot + offsets < slot_count
        onehot = ((target[None, :] == targets[:, None]) & is_live[None, :]).astype(jnp.float32)
        return total + jnp.einsum("os,saf->oaf", onehot, product, precision=lax.Precision.HIGHEST)

    groups = (slot_count + group_size - 1) // group_size
    total = lax.fori_loop(
        0, groups, add_group, jnp.zeros((out_blocks, block_size, feat_width), jnp.float32)
    )
    return total.reshape(out_blocks * block_size, feat_width)


def spread_rows(layer_input, tile_values, slot_index, slot_count):
    full_panel = lax.all_gather(layer_input, "row", axis=0, tiled=True)
    partial_value = combine(tile_values, slot_index, slot_count, full_panel, False)
    return lax.psum_scatter(partial_value, "col", scatter_dimension=0, tiled=True)


def spread_cols(layer_input, tile_values, slot_index, slot_count):
    full_panel = lax.all_gather(layer_input, "col", axis=0, tiled=True)
    partial_value = combine(tile_values, slot_index, slot_count, full_panel, True)
    return lax.psum_scatter(partial_value, "row", scatter_dimension=0, tiled=True)


def tiled_local(features, w_first, w_second, block_index, block_count, block_values, cotangent):
    slot_index = block_index[0, 0]
    slot_count = block_count[0, 0]
    tile_values = block_values[0, 0]
    feat_width = features.shape[1]
    first_linear = jnp.dot(features, w_first, preferred_element_type=jnp.float32).astype(
        jnp.bfloat16
    )
    joined = jnp.concatenate([first_linear, cotangent], axis=1)
    summed = spread_cols(joined, tile_values, slot_index, slot_count)
    first_sum = summed[:, :feat_width]
    back_second = summed[:, feat_width:].astype(jnp.bfloat16)
    first_value, act_back = jax.vjp(activate, first_sum)
    first_active = first_value.astype(jnp.bfloat16)
    second_linear = jnp.dot(first_active, w_second, preferred_element_type=jnp.float32).astype(
        jnp.bfloat16
    )
    out_second = spread_rows(second_linear, tile_values, slot_index, slot_count).astype(
        jnp.bfloat16
    )
    second_terms = jnp.einsum(
        "nf,ng->fg", first_active, back_second, preferred_element_type=jnp.float32
    )
    back_act = jnp.einsum("ng,fg->nf", back_second, w_second, preferred_element_type=jnp.float32)
    back_first = act_back(back_act)[0].astype(jnp.bfloat16)
    back_linear = spread_rows(back_first, tile_values, slot_index, slot_count).astype(jnp.bfloat16)
    first_terms = jnp.einsum("nf,ng->fg", features, back_linear, preferred_element_type=jnp.float32)
    grad_first, grad_second = lax.psum((first_terms, second_terms), ("row", "col"))
    return (out_second, grad_first, grad_second)


VMEM_SPEC = pl.BlockSpec(memory_space=pltpu.VMEM)
VMEM_LIMIT = 12 * 1024 * 1024
DENSE_LIMIT = 20 * 1024 * 1024
SMALL_LIMIT = 2 * 1024 * 1024


class Sizes:
    def __init__(self, mesh, features, block_values):
        self.n_row, self.n_col = mesh.shape["row"], mesh.shape["col"]
        self.n_dev = self.n_row * self.n_col
        self.rows, self.width = features.shape[0] // self.n_dev, features.shape[1]
        self.slots, self.block = block_values.shape[2], block_values.shape[-1]
        self.live = self.slots // 4
        self.nodes = features.shape[0]
        self.blk_rows = self.nodes // self.n_row // self.block
        self.blk_cols = self.nodes // self.n_col // self.block
        self.chunks = self.width // self.block
        self.part = self.chunks * self.rows
        self.at_cot = self.part
        self.at_val = 2 * self.part
        self.at_info = self.at_val + self.live * self.block
        self.payload = self.at_info + 16
        self.n_blocks = self.nodes // self.block

    def replicates(self):
        whole = self.n_dev * self.payload * self.block * 2
        return (
            whole <= REPLICATE_BYTES
            and self.n_col == 4
            and self.n_row % 2 == 0
            and self.n_row & (self.n_row - 1) == 0
            and self.n_row >= 4
            and 2 * self.rows == self.block
            and self.blk_rows == 2
            and self.n_blocks % 2 == 0
        )


def pack_kernel(
    sz, index_ref, count_ref, feat_ref, cot_ref, val_ref, out_ref, index_s, small_sems, sems
):
    small = [
        pltpu.make_async_copy(index_ref, index_s, small_sems.at[0]),
    ]
    for copy in small:
        copy.start()
    copies = []
    for k in range(sz.chunks):
        lanes = pl.ds(k * sz.block, sz.block)
        copies.append((feat_ref.at[:, lanes], k * sz.rows, sz.rows))
        copies.append((cot_ref.at[:, lanes], sz.at_cot + k * sz.rows, sz.rows))
    for s in range(sz.live):
        copies.append((val_ref.at[0, 0, s], sz.at_val + s * sz.block, sz.block))
    copies = [
        pltpu.make_async_copy(src, out_ref.at[pl.ds(at, rows)], sems.at[n])
        for n, (src, at, rows) in enumerate(copies)
    ]
    for copy in copies:
        copy.start()
    for copy in small:
        copy.wait()
    lane = lax.broadcasted_iota(jnp.int32, (16, sz.block), 1)
    info = jnp.where(lane == 0, count_ref[0, 0], 0)
    for s in range(sz.live):
        info = jnp.where(lane == s + 1, index_s[0, 0, s], info)
    out_ref[pl.ds(sz.at_info, 16), :] = info.astype(jnp.float32).astype(jnp.bfloat16)
    for copy in copies:
        copy.wait()


def pack(sz, features, block_index, block_count, block_values, cotangent):
    far = pl.BlockSpec(memory_space=pl.ANY)
    return pl.pallas_call(
        functools.partial(pack_kernel, sz),
        out_shape=pltpu.VMEM((sz.payload, sz.block), jnp.bfloat16),
        in_specs=[far, pl.BlockSpec(memory_space=pltpu.SMEM), far, far, far],
        out_specs=VMEM_SPEC,
        scratch_shapes=[
            pltpu.SMEM(block_index.shape, jnp.int32),
            pltpu.SemaphoreType.DMA((1,)),
            pltpu.SemaphoreType.DMA((2 * sz.chunks + sz.live,)),
        ],
        compiler_params=pltpu.CompilerParams(vmem_limit_bytes=SMALL_LIMIT),
    )(
        pltpu.with_memory_space_constraint(block_index, pltpu.HBM),
        block_count,
        *(
            pltpu.with_memory_space_constraint(a, pltpu.HBM)
            for a in (features, cotangent, block_values)
        ),
    )


def hold(value, token):
    return pl.pallas_call(
        lambda value_ref, token_ref, out_ref: None,
        out_shape=pltpu.VMEM(value.shape, value.dtype),
        in_specs=[VMEM_SPEC, pl.BlockSpec(memory_space=pl.ANY)],
        out_specs=VMEM_SPEC,
        input_output_aliases={0: 0},
        compiler_params=pltpu.CompilerParams(vmem_limit_bytes=SMALL_LIMIT),
    )(pltpu.with_memory_space_constraint(value, pltpu.VMEM), token)


def collect(sz, payload, w_first):
    n_z = sz.n_row // 2

    def send(value, to):
        pairs = []
        for z in range(n_z):
            for y in range(2):
                for x in range(2):
                    for c in range(2):
                        z2, y2, x2, c2 = to(z, y, x, c)
                        src = (z * 2 + y) * 4 + x * 2 + c
                        pairs.append((src, (z2 * 2 + y2) * 4 + x2 * 2 + c2))
        return lax.ppermute(value, AXES, pairs)

    def first_way(z, y, x, c):
        return (z, y, 1 - x, c) if c == 0 else (z, 1 - y, x, c)

    def second_way(z, y, x, c):
        return (z, 1 - y, x, c) if c == 0 else (z, y, 1 - x, c)

    def sibling(z, y, x, c):
        return (z, y, x, 1 - c)

    def flip(d):
        return lambda z, y, x, c: (z ^ d, y, x, c)

    def pair(a, b):
        return jnp.concatenate([a, b], axis=0)

    def plane(near, far):
        return near, far, send(near, sibling), send(far, sibling)

    one = send(payload, first_way)
    near = pair(payload, one)
    planes = [(near, send(near, second_way))]
    near = send(near, flip(1))
    planes.append((near, send(near, second_way)))
    sums, token, w1t = init(sz, w_first, one)

    low = 2
    while low < n_z:
        own = hold(send(payload, flip(2 * low - 1)), token)
        one = send(own, first_way)
        near = pair(own, one)
        planes.append((near, pair(send(own, second_way), send(one, second_way))))
        for d in range(1, low):
            passed = send(near, flip(d))
            planes.append((passed, send(passed, second_way)))
        low *= 2

    sums, info, vals = add_plane(sz, plane(*planes[0]), sums, True)
    token = info
    for near, far in planes[1:-1]:
        sums, token = add_plane(sz, plane(near, far), sums, False)
    near, far = planes[-1]
    sums, token = add_plane(sz, plane(near, hold(far, token)), sums, False)
    return sums, vals, info, w1t


def place():
    row, col = lax.axis_index("row"), lax.axis_index("col")
    return row // 2, row % 2, col // 2, col % 2


def plane_kernel(sz, first, *refs):
    parts, refs = refs[:4], refs[4:]
    sums, info_v = refs[1:3]
    vals_out = refs[3] if first else None
    buf, info_s, turned, sem = refs[-4:]
    _, _, x, c = place()
    block, size = sz.block, sz.payload

    for mine in range(2):

        @pl.when(c == mine)
        def _():
            for q in range(2):
                for n in range(4):
                    core = mine if q == 0 else 1 - mine
                    m = n if core == 0 else (n // 2) + 2 * (n % 2)
                    buf[m, core] = parts[2 * q + n // 2][pl.ds((n % 2) * size, size), :]

    line = lax.broadcasted_iota(jnp.int32, (8, block), 0)
    info = jnp.zeros((8, block), jnp.int32)
    for m in range(4):
        for e in range(2):
            rows = buf[m, e, pl.ds(sz.at_info, 16), :].astype(jnp.float32).astype(jnp.int32)
            info = jnp.where(line == 2 * m + e, rows[0:8], info)
    info_v[...] = info
    info_copy = pltpu.make_async_copy(info_v, info_s, sem)
    info_copy.start()

    if first:
        for m in range(2):
            for e in range(2):
                vals_out[2 * m + e] = buf[m, e, pl.ds(sz.at_val, sz.live * block), :]

    for m in range(4):
        dx, dy = m % 2, m // 2
        for k in range(2 * sz.chunks):
            at = pl.ds(k * sz.rows, sz.rows)
            piece = jnp.concatenate([buf[m, 0, at, :], buf[m, 1, at, :]], axis=0)
            turned[2 * dy + (x ^ dx), pl.ds(k * block, block), :] = jnp.transpose(piece)
    info_copy.wait()

    for m in range(4):
        dx, dy = m % 2, m // 2
        for e in range(2):
            j = (x ^ dx) * 2 + e
            count = info_s[2 * m + e, 0]

            def product(s):
                p = info_s[2 * m + e, s + 1]
                value = buf[m, e, pl.ds(sz.at_val + s * block, block), :]
                return j * sz.blk_cols + lax.rem(p, sz.blk_cols), jnp.dot(
                    turned[2 * dy + p // sz.blk_cols], value, preferred_element_type=jnp.float32
                )

            for s in range(0, sz.live, 2):

                @pl.when(s + 1 == count)
                def _():
                    at, term = product(s)
                    sums[at] += term

                @pl.when(s + 1 < count)
                def _():
                    (at, term), (next_at, next_term) = product(s), product(s + 1)
                    sums[at] += term
                    sums[next_at] += next_term


def dense_kernel(
    sz, sums, vals, info_v, w1t, w2_ref, out_ref, gf_ref, gs_ref, act, rows_out, info_s, sems, *wide
):
    block, width = sz.block, sz.width
    _, _, x, c = place()
    info_copy = pltpu.make_async_copy(info_v, info_s, sems.at[0])
    info_copy.start()
    nt = (((1,), (1,)), ((), ()))
    all_g, all_b, all_a, all_f, gs, gf = wide

    for n in range(sz.n_blocks // 2):
        lanes = pl.ds(2 * n * block, 2 * block)
        both = jnp.concatenate(
            [sums[2 * n].astype(jnp.bfloat16), sums[2 * n + 1].astype(jnp.bfloat16)], axis=1
        )
        g, b = both[:width], both[width:]
        all_g[:, lanes] = g
        all_b[:, lanes] = b
        v = jnp.dot(w1t[...], g, preferred_element_type=jnp.float32)
        p = GELU_C + (GELU_C * GELU_A) * (v * v)
        half = 0.5 + 0.5 * jnp.tanh(v * p)
        value = v * half
        slope = half + (value * (1.0 - half)) * (6.0 * p - 4.0 * GELU_C)
        a = value.astype(jnp.bfloat16)
        act[2 * n] = a[:, :block]
        act[2 * n + 1] = a[:, block:]
        all_a[:, lanes] = a
        back = jnp.dot(w2_ref[...], b, preferred_element_type=jnp.float32)
        all_f[:, lanes] = (back * slope).astype(jnp.bfloat16)

    gs[...] = lax.dot_general(all_a[...], all_b[...], nt, preferred_element_type=jnp.float32)
    gs_copy = pltpu.make_async_copy(gs, gs_ref, sems.at[1])
    gs_copy.start()
    gf[...] = lax.dot_general(all_g[...], all_f[...], nt, preferred_element_type=jnp.float32)
    gf_copy = pltpu.make_async_copy(gf, gf_ref, sems.at[2])
    gf_copy.start()
    info_copy.wait()

    rows_out[...] = jnp.zeros_like(rows_out)
    for dx in range(2):
        for e in range(2):
            q = 2 * dx + e
            count = info_s[q, 0]
            for s in range(sz.live):
                p = info_s[q, s + 1]

                @pl.when((s < count) & (p // sz.blk_cols == x))
                def _():
                    cb = ((x ^ dx) * 2 + e) * sz.blk_cols + lax.rem(p, sz.blk_cols)
                    rows_out[...] += lax.dot_general(
                        act[cb],
                        vals[q, pl.ds(s * block, block), :],
                        nt,
                        preferred_element_type=jnp.float32,
                    )

    h = jnp.transpose(rows_out[...])
    high = h.astype(jnp.bfloat16)
    low = (h - high.astype(jnp.float32)).astype(jnp.bfloat16)
    out = jnp.dot(high, w2_ref[...], preferred_element_type=jnp.float32)
    out += jnp.dot(low, w2_ref[...], preferred_element_type=jnp.float32)
    out = jnp.where(c == 0, out[: sz.rows], out[sz.rows :])
    out_ref[...] = out.astype(jnp.bfloat16)
    gs_copy.wait()
    gf_copy.wait()


def init_kernel(w1_ref, dep_ref, sums, token, w1t):
    sums[...] = jnp.zeros_like(sums)
    token[...] = jnp.zeros_like(token)
    w1t[...] = jnp.transpose(w1_ref[...])


def init(sz, w_first, dep):
    return pl.pallas_call(
        init_kernel,
        out_shape=(
            pltpu.VMEM((sz.n_blocks, 2 * sz.width, sz.block), jnp.float32),
            pltpu.VMEM((8, sz.block), jnp.int32),
            pltpu.VMEM((sz.width, sz.width), jnp.bfloat16),
        ),
        in_specs=[VMEM_SPEC, pl.BlockSpec(memory_space=pl.ANY)],
        out_specs=[VMEM_SPEC] * 3,
        compiler_params=pltpu.CompilerParams(vmem_limit_bytes=SMALL_LIMIT),
    )(w_first, dep)


def add_plane(sz, parts, sums, first):
    parts = [pltpu.with_memory_space_constraint(a, pltpu.VMEM) for a in (*parts, sums)]
    out_shape = [
        pltpu.VMEM((sz.n_blocks, 2 * sz.width, sz.block), jnp.float32),
        pltpu.VMEM((8, sz.block), jnp.int32),
    ]
    if first:
        out_shape.append(pltpu.VMEM((4, sz.live * sz.block, sz.block), jnp.bfloat16))
    return pl.pallas_call(
        functools.partial(plane_kernel, sz, first),
        out_shape=tuple(out_shape),
        in_specs=[VMEM_SPEC] * 5,
        out_specs=[VMEM_SPEC] * len(out_shape),
        input_output_aliases={4: 0},
        scratch_shapes=[
            pltpu.VMEM((4, 2, sz.payload, sz.block), jnp.bfloat16),
            pltpu.SMEM((8, sz.block), jnp.int32),
            pltpu.VMEM((4, 2 * sz.width, sz.block), jnp.bfloat16),
            pltpu.SemaphoreType.DMA,
        ],
        compiler_params=pltpu.CompilerParams(vmem_limit_bytes=VMEM_LIMIT),
    )(*parts)


def dense(sz, sums, vals, info, w1t, w_second):
    grad = jax.ShapeDtypeStruct((sz.width, sz.width), jnp.float32)
    inputs = [pltpu.with_memory_space_constraint(a, pltpu.VMEM) for a in (sums, vals, info, w1t)]
    far = pl.BlockSpec(memory_space=pl.ANY)
    return tuple(
        pl.pallas_call(
            functools.partial(dense_kernel, sz),
            out_shape=(jax.ShapeDtypeStruct((sz.rows, sz.width), jnp.bfloat16), grad, grad),
            in_specs=[VMEM_SPEC] * 5,
            out_specs=[VMEM_SPEC, far, far],
            scratch_shapes=[
                pltpu.VMEM((sz.n_blocks, sz.width, sz.block), jnp.bfloat16),
                pltpu.VMEM((sz.width, sz.block), jnp.float32),
                pltpu.SMEM((8, sz.block), jnp.int32),
                pltpu.SemaphoreType.DMA((3,)),
            ]
            + [pltpu.VMEM((sz.width, sz.nodes), jnp.bfloat16)] * 4
            + [pltpu.VMEM((sz.width, sz.width), jnp.float32)] * 2,
            compiler_params=pltpu.CompilerParams(vmem_limit_bytes=DENSE_LIMIT),
        )(*inputs, w_second)
    )


def replicated_local(sz, features, w_first, w_second, block_index, block_count, block_values, cotangent):
    payload = pack(sz, features, block_index, block_count, block_values, cotangent)
    sums, vals, info, w1t = collect(sz, payload, w_first)
    return dense(sz, sums, vals, info, w1t, w_second)


def solution(mesh):
    specs = dict(
        mesh=mesh,
        in_specs=(
            P(("row", "col"), None),
            P(),
            P(),
            P("row", "col", None),
            P("row", "col"),
            P("row", "col", None, None, None),
            P(("row", "col"), None),
        ),
        out_specs=(P(("row", "col"), None), P(), P()),
        check_vma=False,
    )

    def run(features, w_first, w_second, block_index, block_count, block_values, cotangent):
        sz = Sizes(mesh, features, block_values)
        local = functools.partial(replicated_local, sz) if sz.replicates() else tiled_local
        return jax.shard_map(local, **specs)(
            features, w_first, w_second, block_index, block_count, block_values, cotangent
        )

    return run
```

```python
import functools
import math

import jax
import jax.numpy as jnp
from jax import lax
from jax.experimental import pallas as pl
from jax.experimental.pallas import tpu as pltpu
from jax.sharding import PartitionSpec as P

AXES = ("row", "col")
GELU_C = 0.7978845608028654
GELU_A = 0.044715
REPLICATE_BYTES = 8 * 1024 * 1024


def activate(v):
    return jax.nn.gelu(v, approximate=True)


def combine(tile_values, slot_index, slot_count, full_panel, flip):
    slots = slot_index.shape[0]
    block_size = tile_values.shape[-1]
    feat_width = full_panel.shape[1]
    in_blocks = full_panel.shape[0] // block_size
    if flip:
        col_blocks = slots // in_blocks
        out_blocks = col_blocks
    else:
        col_blocks = in_blocks
        out_blocks = slots // in_blocks
    group_size = math.gcd(slots, 32)
    panel_blocks = full_panel.reshape(in_blocks, block_size, feat_width)
    targets = jnp.arange(out_blocks, dtype=jnp.int32)
    offsets = jnp.arange(group_size, dtype=jnp.int32)

    def add_group(group_no, total):
        first_slot = group_no * group_size
        slot_ids = lax.dynamic_slice_in_dim(slot_index, first_slot, group_size, 0)
        group_values = lax.dynamic_slice_in_dim(tile_values, first_slot, group_size, 0)
        block_row = slot_ids // col_blocks
        block_col = slot_ids % col_blocks
        if flip:
            picked = panel_blocks[block_row]
            product = jnp.einsum(
                "sab,saf->sbf", group_values, picked, preferred_element_type=jnp.float32
            )
            target = block_col
        else:
            picked = panel_blocks[block_col]
            product = jnp.einsum(
                "sab,sbf->saf", group_values, picked, preferred_element_type=jnp.float32
            )
            target = block_row
        is_live = first_slot + offsets < slot_count
        onehot = ((target[None, :] == targets[:, None]) & is_live[None, :]).astype(jnp.float32)
        return total + jnp.einsum("os,saf->oaf", onehot, product, precision=lax.Precision.HIGHEST)

    groups = (slot_count + group_size - 1) // group_size
    total = lax.fori_loop(
        0, groups, add_group, jnp.zeros((out_blocks, block_size, feat_width), jnp.float32)
    )
    return total.reshape(out_blocks * block_size, feat_width)


def spread_rows(layer_input, tile_values, slot_index, slot_count):
    full_panel = lax.all_gather(layer_input, "row", axis=0, tiled=True)
    partial_value = combine(tile_values, slot_index, slot_count, full_panel, False)
    return lax.psum_scatter(partial_value, "col", scatter_dimension=0, tiled=True)


def spread_cols(layer_input, tile_values, slot_index, slot_count):
    full_panel = lax.all_gather(layer_input, "col", axis=0, tiled=True)
    partial_value = combine(tile_values, slot_index, slot_count, full_panel, True)
    return lax.psum_scatter(partial_value, "row", scatter_dimension=0, tiled=True)


def tiled_local(features, w_first, w_second, block_index, block_count, block_values, cotangent):
    slot_index = block_index[0, 0]
    slot_count = block_count[0, 0]
    tile_values = block_values[0, 0]
    feat_width = features.shape[1]
    first_linear = jnp.dot(features, w_first, preferred_element_type=jnp.float32).astype(
        jnp.bfloat16
    )
    joined = jnp.concatenate([first_linear, cotangent], axis=1)
    summed = spread_cols(joined, tile_values, slot_index, slot_count)
    first_sum = summed[:, :feat_width]
    back_second = summed[:, feat_width:].astype(jnp.bfloat16)
    first_value, act_back = jax.vjp(activate, first_sum)
    first_active = first_value.astype(jnp.bfloat16)
    second_linear = jnp.dot(first_active, w_second, preferred_element_type=jnp.float32).astype(
        jnp.bfloat16
    )
    out_second = spread_rows(second_linear, tile_values, slot_index, slot_count).astype(
        jnp.bfloat16
    )
    second_terms = jnp.einsum(
        "nf,ng->fg", first_active, back_second, preferred_element_type=jnp.float32
    )
    back_act = jnp.einsum("ng,fg->nf", back_second, w_second, preferred_element_type=jnp.float32)
    back_first = act_back(back_act)[0].astype(jnp.bfloat16)
    back_linear = spread_rows(back_first, tile_values, slot_index, slot_count).astype(jnp.bfloat16)
    first_terms = jnp.einsum("nf,ng->fg", features, back_linear, preferred_element_type=jnp.float32)
    grad_first, grad_second = lax.psum((first_terms, second_terms), ("row", "col"))
    return (out_second, grad_first, grad_second)


VMEM_SPEC = pl.BlockSpec(memory_space=pltpu.VMEM)
VMEM_LIMIT = 12 * 1024 * 1024
DENSE_LIMIT = 20 * 1024 * 1024
SMALL_LIMIT = 2 * 1024 * 1024


class Sizes:
    def __init__(self, mesh, features, block_values):
        self.n_row, self.n_col = mesh.shape["row"], mesh.shape["col"]
        self.n_dev = self.n_row * self.n_col
        self.rows, self.width = features.shape[0] // self.n_dev, features.shape[1]
        self.slots, self.block = block_values.shape[2], block_values.shape[-1]
        self.live = self.slots // 4
        self.nodes = features.shape[0]
        self.blk_rows = self.nodes // self.n_row // self.block
        self.blk_cols = self.nodes // self.n_col // self.block
        self.chunks = self.width // self.block
        self.part = self.chunks * self.rows
        self.at_cot = self.part
        self.at_val = 2 * self.part
        self.at_info = self.at_val + self.live * self.block
        self.payload = self.at_info + 16
        self.n_blocks = self.nodes // self.block

    def replicates(self):
        whole = self.n_dev * self.payload * self.block * 2
        return (
            whole <= REPLICATE_BYTES
            and self.n_col == 4
            and self.n_row % 2 == 0
            and self.n_row & (self.n_row - 1) == 0
            and self.n_row >= 4
            and 2 * self.rows == self.block
            and self.blk_rows == 2
            and self.n_blocks % 2 == 0
        )


def pack_kernel(
    sz, index_ref, count_ref, feat_ref, cot_ref, val_ref, out_ref, index_s, small_sems, sems
):
    small = [
        pltpu.make_async_copy(index_ref, index_s, small_sems.at[0]),
    ]
    for copy in small:
        copy.start()
    copies = []
    for k in range(sz.chunks):
        lanes = pl.ds(k * sz.block, sz.block)
        copies.append((feat_ref.at[:, lanes], k * sz.rows, sz.rows))
        copies.append((cot_ref.at[:, lanes], sz.at_cot + k * sz.rows, sz.rows))
    for s in range(sz.live):
        copies.append((val_ref.at[0, 0, s], sz.at_val + s * sz.block, sz.block))
    copies = [
        pltpu.make_async_copy(src, out_ref.at[pl.ds(at, rows)], sems.at[n])
        for n, (src, at, rows) in enumerate(copies)
    ]
    for copy in copies:
        copy.start()
    for copy in small:
        copy.wait()
    lane = lax.broadcasted_iota(jnp.int32, (16, sz.block), 1)
    info = jnp.where(lane == 0, count_ref[0, 0], 0)
    for s in range(sz.live):
        info = jnp.where(lane == s + 1, index_s[0, 0, s], info)
    out_ref[pl.ds(sz.at_info, 16), :] = info.astype(jnp.float32).astype(jnp.bfloat16)
    for copy in copies:
        copy.wait()


def pack(sz, features, block_index, block_count, block_values, cotangent):
    far = pl.BlockSpec(memory_space=pl.ANY)
    return pl.pallas_call(
        functools.partial(pack_kernel, sz),
        out_shape=pltpu.VMEM((sz.payload, sz.block), jnp.bfloat16),
        in_specs=[far, pl.BlockSpec(memory_space=pltpu.SMEM), far, far, far],
        out_specs=VMEM_SPEC,
        scratch_shapes=[
            pltpu.SMEM(block_index.shape, jnp.int32),
            pltpu.SemaphoreType.DMA((1,)),
            pltpu.SemaphoreType.DMA((2 * sz.chunks + sz.live,)),
        ],
        compiler_params=pltpu.CompilerParams(vmem_limit_bytes=SMALL_LIMIT),
    )(
        pltpu.with_memory_space_constraint(block_index, pltpu.HBM),
        block_count,
        *(
            pltpu.with_memory_space_constraint(a, pltpu.HBM)
            for a in (features, cotangent, block_values)
        ),
    )


def hold(value, token):
    return pl.pallas_call(
        lambda value_ref, token_ref, out_ref: None,
        out_shape=pltpu.VMEM(value.shape, value.dtype),
        in_specs=[VMEM_SPEC, pl.BlockSpec(memory_space=pl.ANY)],
        out_specs=VMEM_SPEC,
        input_output_aliases={0: 0},
        compiler_params=pltpu.CompilerParams(vmem_limit_bytes=SMALL_LIMIT),
    )(pltpu.with_memory_space_constraint(value, pltpu.VMEM), token)


def collect(sz, payload, w_first):
    n_z = sz.n_row // 2

    def send(value, to):
        pairs = []
        for z in range(n_z):
            for y in range(2):
                for x in range(2):
                    for c in range(2):
                        z2, y2, x2, c2 = to(z, y, x, c)
                        src = (z * 2 + y) * 4 + x * 2 + c
                        pairs.append((src, (z2 * 2 + y2) * 4 + x2 * 2 + c2))
        return lax.ppermute(value, AXES, pairs)

    def first_way(z, y, x, c):
        return (z, y, 1 - x, c) if c == 0 else (z, 1 - y, x, c)

    def second_way(z, y, x, c):
        return (z, 1 - y, x, c) if c == 0 else (z, y, 1 - x, c)

    def sibling(z, y, x, c):
        return (z, y, x, 1 - c)

    def flip(d):
        return lambda z, y, x, c: (z ^ d, y, x, c)

    def pair(a, b):
        return jnp.concatenate([a, b], axis=0)

    def plane(near, far):
        return near, far, send(near, sibling), send(far, sibling)

    one = send(payload, first_way)
    near = pair(payload, one)
    planes = [(near, send(near, second_way))]
    near = send(near, flip(1))
    planes.append((near, send(near, second_way)))
    sums, token, w1t = init(sz, w_first, payload)

    low = 2
    while low < n_z:
        own = hold(send(payload, flip(2 * low - 1)), token)
        one = send(own, first_way)
        near = pair(own, one)
        planes.append((near, pair(send(own, second_way), send(one, second_way))))
        for d in range(1, low):
            passed = send(near, flip(d))
            planes.append((passed, send(passed, second_way)))
        low *= 2

    sums, info, vals = add_plane(sz, plane(*planes[0]), sums, True)
    token = info
    for near, far in planes[1:-1]:
        sums, token = add_plane(sz, plane(near, far), sums, False)
    near, far = planes[-1]
    sums, token = add_plane(sz, plane(near, hold(far, token)), sums, False)
    return sums, vals, info, w1t


def place():
    row, col = lax.axis_index("row"), lax.axis_index("col")
    return row // 2, row % 2, col // 2, col % 2


def plane_kernel(sz, first, *refs):
    parts, refs = refs[:4], refs[4:]
    sums, info_v = refs[1:3]
    vals_out = refs[3] if first else None
    buf, info_s, turned, sem = refs[-4:]
    _, _, x, c = place()
    block, size = sz.block, sz.payload

    for mine in range(2):

        @pl.when(c == mine)
        def _():
            for q in range(2):
                for n in range(4):
                    core = mine if q == 0 else 1 - mine
                    m = n if core == 0 else (n // 2) + 2 * (n % 2)
                    buf[m, core] = parts[2 * q + n // 2][pl.ds((n % 2) * size, size), :]

    line = lax.broadcasted_iota(jnp.int32, (8, block), 0)
    info = jnp.zeros((8, block), jnp.int32)
    for m in range(4):
        for e in range(2):
            rows = buf[m, e, pl.ds(sz.at_info, 16), :].astype(jnp.float32).astype(jnp.int32)
            info = jnp.where(line == 2 * m + e, rows[0:8], info)
    info_v[...] = info
    info_copy = pltpu.make_async_copy(info_v, info_s, sem)
    info_copy.start()

    if first:
        for m in range(2):
            for e in range(2):
                vals_out[2 * m + e] = buf[m, e, pl.ds(sz.at_val, sz.live * block), :]

    for m in range(4):
        dx, dy = m % 2, m // 2
        for k in range(2 * sz.chunks):
            at = pl.ds(k * sz.rows, sz.rows)
            piece = jnp.concatenate([buf[m, 0, at, :], buf[m, 1, at, :]], axis=0)
            turned[2 * dy + (x ^ dx), pl.ds(k * block, block), :] = jnp.transpose(piece)
    info_copy.wait()

    for m in range(4):
        dx, dy = m % 2, m // 2
        for e in range(2):
            j = (x ^ dx) * 2 + e
            count = info_s[2 * m + e, 0]

            def product(s):
                p = info_s[2 * m + e, s + 1]
                value = buf[m, e, pl.ds(sz.at_val + s * block, block), :]
                return j * sz.blk_cols + lax.rem(p, sz.blk_cols), jnp.dot(
                    turned[2 * dy + p // sz.blk_cols], value, preferred_element_type=jnp.float32
                )

            for s in range(0, sz.live, 2):

                @pl.when(s + 1 == count)
                def _():
                    at, term = product(s)
                    sums[at] += term

                @pl.when(s + 1 < count)
                def _():
                    (at, term), (next_at, next_term) = product(s), product(s + 1)
                    sums[at] += term
                    sums[next_at] += next_term


def dense_kernel(
    sz, sums, vals, info_v, w1t, w2_ref, out_ref, gf_ref, gs_ref, act, rows_out, info_s, sems, *wide
):
    block, width = sz.block, sz.width
    _, _, x, c = place()
    info_copy = pltpu.make_async_copy(info_v, info_s, sems.at[0])
    info_copy.start()
    nt = (((1,), (1,)), ((), ()))
    all_g, all_b, all_a, all_f, gs, gf = wide

    for n in range(sz.n_blocks // 2):
        lanes = pl.ds(2 * n * block, 2 * block)
        both = jnp.concatenate(
            [sums[2 * n].astype(jnp.bfloat16), sums[2 * n + 1].astype(jnp.bfloat16)], axis=1
        )
        g, b = both[:width], both[width:]
        all_g[:, lanes] = g
        all_b[:, lanes] = b
        v = jnp.dot(w1t[...], g, preferred_element_type=jnp.float32)
        p = GELU_C + (GELU_C * GELU_A) * (v * v)
        half = 0.5 + 0.5 * jnp.tanh(v * p)
        value = v * half
        slope = half + (value * (1.0 - half)) * (6.0 * p - 4.0 * GELU_C)
        a = value.astype(jnp.bfloat16)
        act[2 * n] = a[:, :block]
        act[2 * n + 1] = a[:, block:]
        all_a[:, lanes] = a
        back = jnp.dot(w2_ref[...], b, preferred_element_type=jnp.float32)
        all_f[:, lanes] = (back * slope).astype(jnp.bfloat16)

    for at in range(0, width, width // 2):
        gs[:, at : at + width // 2] = lax.dot_general(
            all_a[...], all_b[at : at + width // 2, :], nt, preferred_element_type=jnp.float32
        )
    gs_copy = pltpu.make_async_copy(gs, gs_ref, sems.at[1])
    gs_copy.start()
    for at in range(0, width, width // 2):
        gf[:, at : at + width // 2] = lax.dot_general(
            all_g[...], all_f[at : at + width // 2, :], nt, preferred_element_type=jnp.float32
        )
    gf_copy = pltpu.make_async_copy(gf, gf_ref, sems.at[2])
    gf_copy.start()
    info_copy.wait()

    rows_out[...] = jnp.zeros_like(rows_out)
    for dx in range(2):
        for e in range(2):
            q = 2 * dx + e
            count = info_s[q, 0]
            for s in range(sz.live):
                p = info_s[q, s + 1]

                @pl.when((s < count) & (p // sz.blk_cols == x))
                def _():
                    cb = ((x ^ dx) * 2 + e) * sz.blk_cols + lax.rem(p, sz.blk_cols)
                    rows_out[...] += lax.dot_general(
                        act[cb],
                        vals[q, pl.ds(s * block, block), :],
                        nt,
                        preferred_element_type=jnp.float32,
                    )

    h = jnp.transpose(rows_out[...])
    high = h.astype(jnp.bfloat16)
    low = (h - high.astype(jnp.float32)).astype(jnp.bfloat16)
    out = jnp.dot(high, w2_ref[...], preferred_element_type=jnp.float32)
    out += jnp.dot(low, w2_ref[...], preferred_element_type=jnp.float32)
    out = jnp.where(c == 0, out[: sz.rows], out[sz.rows :])
    out_ref[...] = out.astype(jnp.bfloat16)
    gs_copy.wait()
    gf_copy.wait()


def init_kernel(w1_ref, dep_ref, sums, token, w1t):
    sums[...] = jnp.zeros_like(sums)
    token[...] = jnp.zeros_like(token)
    w1t[...] = jnp.transpose(w1_ref[...])


def init(sz, w_first, dep):
    return pl.pallas_call(
        init_kernel,
        out_shape=(
            pltpu.VMEM((sz.n_blocks, 2 * sz.width, sz.block), jnp.float32),
            pltpu.VMEM((8, sz.block), jnp.int32),
            pltpu.VMEM((sz.width, sz.width), jnp.bfloat16),
        ),
        in_specs=[VMEM_SPEC, pl.BlockSpec(memory_space=pl.ANY)],
        out_specs=[VMEM_SPEC] * 3,
        compiler_params=pltpu.CompilerParams(vmem_limit_bytes=SMALL_LIMIT),
    )(w_first, dep)


def add_plane(sz, parts, sums, first):
    parts = [pltpu.with_memory_space_constraint(a, pltpu.VMEM) for a in (*parts, sums)]
    out_shape = [
        pltpu.VMEM((sz.n_blocks, 2 * sz.width, sz.block), jnp.float32),
        pltpu.VMEM((8, sz.block), jnp.int32),
    ]
    if first:
        out_shape.append(pltpu.VMEM((4, sz.live * sz.block, sz.block), jnp.bfloat16))
    return pl.pallas_call(
        functools.partial(plane_kernel, sz, first),
        out_shape=tuple(out_shape),
        in_specs=[VMEM_SPEC] * 5,
        out_specs=[VMEM_SPEC] * len(out_shape),
        input_output_aliases={4: 0},
        scratch_shapes=[
            pltpu.VMEM((4, 2, sz.payload, sz.block), jnp.bfloat16),
            pltpu.SMEM((8, sz.block), jnp.int32),
            pltpu.VMEM((4, 2 * sz.width, sz.block), jnp.bfloat16),
            pltpu.SemaphoreType.DMA,
        ],
        compiler_params=pltpu.CompilerParams(vmem_limit_bytes=VMEM_LIMIT),
    )(*parts)


def dense(sz, sums, vals, info, w1t, w_second):
    grad = jax.ShapeDtypeStruct((sz.width, sz.width), jnp.float32)
    inputs = [pltpu.with_memory_space_constraint(a, pltpu.VMEM) for a in (sums, vals, info, w1t)]
    far = pl.BlockSpec(memory_space=pl.ANY)
    return tuple(
        pl.pallas_call(
            functools.partial(dense_kernel, sz),
            out_shape=(jax.ShapeDtypeStruct((sz.rows, sz.width), jnp.bfloat16), grad, grad),
            in_specs=[VMEM_SPEC] * 5,
            out_specs=[VMEM_SPEC, far, far],
            scratch_shapes=[
                pltpu.VMEM((sz.n_blocks, sz.width, sz.block), jnp.bfloat16),
                pltpu.VMEM((sz.width, sz.block), jnp.float32),
                pltpu.SMEM((8, sz.block), jnp.int32),
                pltpu.SemaphoreType.DMA((3,)),
            ]
            + [pltpu.VMEM((sz.width, sz.nodes), jnp.bfloat16)] * 4
            + [pltpu.VMEM((sz.width, sz.width), jnp.float32)] * 2,
            compiler_params=pltpu.CompilerParams(vmem_limit_bytes=DENSE_LIMIT),
        )(*inputs, w_second)
    )


def replicated_local(sz, features, w_first, w_second, block_index, block_count, block_values, cotangent):
    payload = pack(sz, features, block_index, block_count, block_values, cotangent)
    sums, vals, info, w1t = collect(sz, payload, w_first)
    return dense(sz, sums, vals, info, w1t, w_second)


def solution(mesh):
    specs = dict(
        mesh=mesh,
        in_specs=(
            P(("row", "col"), None),
            P(),
            P(),
            P("row", "col", None),
            P("row", "col"),
            P("row", "col", None, None, None),
            P(("row", "col"), None),
        ),
        out_specs=(P(("row", "col"), None), P(), P()),
        check_vma=False,
    )

    def run(features, w_first, w_second, block_index, block_count, block_values, cotangent):
        sz = Sizes(mesh, features, block_values)
        local = functools.partial(replicated_local, sz) if sz.replicates() else tiled_local
        return jax.shard_map(local, **specs)(
            features, w_first, w_second, block_index, block_count, block_values, cotangent
        )

    return run
```
